128 devices in a mesh: seq: 16 (over x, y), chan: 8 (over z, core).
Axes of the slice: x: 4, y: 4, z: 4, core: 2. Of those that a mesh axis runs over, the one named last changes fastest.
Arguments:
- tokens: bfloat16 [16384, 1024], P('seq', 'chan'), may hold values from -64 to 64
- norm_gain: float32 [1024], replicated, may hold values from 0.1 to 1.9
- in_weight: bfloat16 [3, 1024, 1024], P(None, None, 'chan'), may hold values from -0.1875 to 0.1875
- short_kernel: float32 [3, 3, 1024], P(None, None, 'chan'), may hold values from -3 to 3
- filter_fwd: float32 [16384, 1024], P('seq', 'chan'), may hold values from -0.75 to 0.75
- filter_bwd: float32 [16384, 1024], P('seq', 'chan'), may hold values from -0.75 to 0.75
- skip_gain: float32 [1024], P('chan'), may hold values from -1 to 1
- out_weight: bfloat16 [1024, 1024], P('chan'), may hold values from -0.1875 to 0.1875
Outputs:
- layer_out: float32 [16384, 1024], P('seq', 'chan')
The draws below stay inside these ranges and needn't reach their ends.
All inputs are finite; a program needn't handle non-finite values.
Results may differ from the reference program's by a relative error of at most 0.0035.
Values may be sent and summed in bfloat16 or wider, within the bound.
No kernel may reach another device: no remote copies, remote signals or barrier semaphores. Data moves between devices by JAX's collectives and lax.ppermute only.
A program may use at most 128 MiB of HBM per device.

```python
import jax
import jax.numpy as jnp
from jax import lax

MODEL_WIDTH = 1024
SEQUENCE_TOKENS = 16384


def draw_tokens(key, part):
    key = jax.random.fold_in(key, 11)
    base_key, row_key, col_key = jax.random.split(key, 3)
    base_values = jax.random.truncated_normal(base_key, -4.0, 4.0, (SEQUENCE_TOKENS, MODEL_WIDTH), jnp.float32)
    row_scale = jnp.exp(jax.random.uniform(row_key, (SEQUENCE_TOKENS, 1), jnp.float32, jnp.log(0.4), jnp.log(4.0)))
    col_scale = jnp.exp(jax.random.uniform(col_key, (1, MODEL_WIDTH), jnp.float32, jnp.log(0.4), jnp.log(4.0)))
    return (base_values * row_scale * col_scale).astype(jnp.bfloat16)


def filter_values(key, tau_low, tau_high):
    jitter_random_key, timescale_random_key, spike_random_key, layer_depth_random_key = jax.random.split(key, 4)
    noise = jax.random.truncated_normal(jitter_random_key, -4.0, 4.0, (SEQUENCE_TOKENS, MODEL_WIDTH), jnp.float32)
    log_tau = jax.random.uniform(timescale_random_key, (1, MODEL_WIDTH), jnp.float32, jnp.log(tau_low), jnp.log(tau_high))
    decay_len = jnp.exp(log_tau)
    amplitude = lax_rsqrt(jnp.minimum(decay_len, float(SEQUENCE_TOKENS)))
    token_offset = jnp.arange(SEQUENCE_TOKENS, dtype=jnp.int32)[:, None]
    decay_profile = jnp.exp(-token_offset.astype(jnp.float32) / decay_len)
    spike_position = jax.random.randint(spike_random_key, (4, MODEL_WIDTH), 0, SEQUENCE_TOKENS)
    spike_keep_mask = jax.random.uniform(layer_depth_random_key, (4, MODEL_WIDTH), jnp.float32, 0.5, 0.8)
    for spike_count in range(4):
        decay_profile = decay_profile * jnp.where(token_offset >= spike_position[spike_count][None, :], spike_keep_mask[spike_count][None, :], 1.0)
    return noise * amplitude * decay_profile


def lax_rsqrt(values):
    return 1.0 / jnp.sqrt(values)


def draw_filter_fwd(key, part):
    key = jax.random.fold_in(key, 23)
    return filter_values(key, 30.0, 4.0 * SEQUENCE_TOKENS)


def draw_filter_bwd(key, part):
    key = jax.random.fold_in(key, 37)
    return filter_values(key, 30.0, 4.0 * SEQUENCE_TOKENS)


def steps_of(rng, shape, shards, least, high):
    factor_of = 1.0
    for axis_at, shards_of in shards:
        heights = jax.random.uniform(jax.random.fold_in(jax.random.fold_in(rng, 6), axis_at), (shards_of,), jnp.float32, least / len(shards), high / len(shards))
        factor_of = factor_of * jnp.repeat(jnp.exp(heights), shape[axis_at] // shards_of).reshape((-1,) + (1,) * (len(shape) - 1 - axis_at))
    return factor_of


def scatter_about(key, shape, width, limit, shards=(), kind=jnp.bfloat16):
    loudness = steps_of(key, shape, shards, -0.22, 0.18) if shards else 1.0
    drawn = jax.random.normal(key, shape, jnp.float32) * width * loudness
    return jnp.minimum(jnp.maximum(drawn, -limit), limit).astype(kind)


def setup_inputs(seed: int = 0) -> dict:
    seeds = jax.random.split(jax.random.key(seed), 9)
    return {
        "tokens": draw_tokens(jax.random.fold_in(seeds[8], 71), 0),
        "norm_gain": jnp.clip(1.0 + 0.18 * jax.random.normal(seeds[1], (MODEL_WIDTH,), jnp.float32), 0.1, 1.9),
        "in_weight": scatter_about(seeds[2], (3, MODEL_WIDTH, MODEL_WIDTH), MODEL_WIDTH ** -0.5, 0.1875, ((2, 8),)),
        "short_kernel": scatter_about(seeds[3], (3, 3, MODEL_WIDTH), 0.6, 3.0, ((2, 8),), jnp.float32),
        "filter_fwd": draw_filter_fwd(jax.random.fold_in(seeds[8], 71), 0),
        "filter_bwd": draw_filter_bwd(jax.random.fold_in(seeds[8], 71), 0),
        "skip_gain": jnp.clip(jax.random.uniform(seeds[6], (MODEL_WIDTH,), jnp.float32, -1.0, 1.0) * steps_of(seeds[6], (MODEL_WIDTH,), ((0, 8),), -0.4, 0.0), -1.0, 1.0),
        "out_weight": scatter_about(seeds[7], (MODEL_WIDTH, MODEL_WIDTH), MODEL_WIDTH ** -0.5, 0.1875, ((0, 8),)),
    }


def reference(tokens, norm_gain, in_weight, short_kernel, filter_fwd, filter_bwd, skip_gain, out_weight):
    widened = tokens.astype(jnp.float32)
    inv_rms = lax.rsqrt(lax.optimization_barrier(jnp.mean(widened * widened, axis=-1, keepdims=True)) + 1e-05)
    normed = (widened * inv_rms * norm_gain).astype(jnp.bfloat16)
    projected = jnp.einsum('td,jde->jte', normed.astype(jnp.float32), in_weight.astype(jnp.float32), precision=lax.Precision.HIGHEST)
    padded = jnp.pad(projected, ((0, 0), (2, 0), (0, 0)))
    short_mix = short_kernel[0][:, None, :] * projected + short_kernel[1][:, None, :] * padded[:, 1:-1, :] + short_kernel[2][:, None, :] * padded[:, :-2, :]
    signal = short_mix[0] * short_mix[1]
    length = signal.shape[0]
    fft_size = 2 * length
    reversed_bwd = jnp.concatenate([jnp.zeros_like(filter_bwd), filter_bwd[::-1]], axis=0)
    filter_spec = jnp.fft.rfft(filter_fwd, n=fft_size, axis=0) + jnp.fft.rfft(reversed_bwd, axis=0)
    spectrum = jnp.fft.rfft(signal, n=fft_size, axis=0) * filter_spec
    long_mix = jnp.fft.irfft(spectrum, n=fft_size, axis=0)[:length] + skip_gain * signal
    gated_out = (short_mix[2] * long_mix).astype(jnp.bfloat16)
    return widened + jnp.dot(gated_out, out_weight, preferred_element_type=jnp.float32)
```

```python
import functools

import jax
import jax.numpy as jnp
import ml_dtypes
import numpy as np
from jax import lax
from jax.experimental import pallas as pl
from jax.experimental.pallas import tpu as pltpu
from jax.sharding import PartitionSpec as P

HALO = 16
LANES = 128
VMEM_LIMIT = 56 * 1024 * 1024
VMEM = pl.BlockSpec(memory_space=pltpu.VMEM)
F32 = jnp.float32
BF16 = jnp.bfloat16


def params():
    return pltpu.CompilerParams(vmem_limit_bytes=VMEM_LIMIT)


def split_np(table):
    high = table.astype(np.float32).astype(ml_dtypes.bfloat16)
    low = (table - high.astype(np.float64)).astype(np.float32).astype(ml_dtypes.bfloat16)
    return high, low


@functools.cache
def tables():
    n = LANES
    period = 2 * n * n
    k = np.arange(n, dtype=np.float64)
    first = 2 * np.pi * np.outer(k + 0.5, k) / (2 * n)
    forward = np.concatenate([np.cos(first), -np.sin(first)], axis=0)
    backward = np.concatenate([np.cos(first).T, -np.sin(first).T], axis=1) * (2.0 / period)
    second = 2 * np.pi * np.outer(k, k) / n
    cosine, sine = np.cos(second), np.sin(second)
    mix = np.block([[cosine, -sine], [sine, cosine]])
    unmix = np.block([[cosine, sine], [-sine, cosine]])
    turn = 2 * np.pi * np.outer(k + 0.5, k) / period
    twiddle = np.stack([np.cos(turn), -np.sin(turn)]).astype(np.float32)
    step = 2 * np.pi * (k[:, None] + 0.5 + 2 * n * k[None, :]) / period
    ahead = np.stack([np.cos(step), np.sin(step)]).astype(np.float32)
    forward_hi, forward_lo = split_np(forward)
    backward_hi, backward_lo = split_np(backward)
    mix_hi, mix_lo = split_np(mix)
    unmix_hi, unmix_lo = split_np(unmix)
    return {
        "forward": np.concatenate([forward_hi, forward_lo, forward_hi], axis=1),
        "backward": np.concatenate([backward_hi, backward_lo, backward_hi], axis=1),
        "mix": np.concatenate([mix_hi, mix_lo], axis=0),
        "unmix": np.concatenate([unmix_hi, unmix_lo], axis=0),
        "twiddle": twiddle,
        "ahead": ahead,
    }


def halves(value):
    high = value.astype(BF16)
    return high, (value - high.astype(F32)).astype(BF16)


def dot(left, right):
    return jnp.dot(left, right, preferred_element_type=F32)


def left_dot(table, value):
    high, low = halves(value)
    return dot(table, jnp.concatenate([high, high, low], axis=0))


def right_dot(value, table_ref):
    high, low = halves(value)
    depth = value.shape[1]
    table_hi = table_ref[:depth]
    return dot(jnp.concatenate([high, low, high], axis=1), jnp.concatenate([table_hi, table_hi, table_ref[depth:]], axis=0))


def transform(pair, forward_ref, mix_ref, twiddle_ref):
    n = LANES
    parts = left_dot(forward_ref[...], jnp.concatenate(pair, axis=1))
    cosine, sine = twiddle_ref[0], twiddle_ref[1]
    rows = []
    for i in range(2):
        real = parts[:n, i * n : (i + 1) * n]
        imag = parts[n:, i * n : (i + 1) * n]
        rows.append(jnp.concatenate([real * cosine - imag * sine, real * sine + imag * cosine], axis=1))
    return right_dot(jnp.concatenate(rows, axis=0), mix_ref)


def spread_kernel(fwd_ref, bwd_ref, out_ref):
    for which, source in enumerate((fwd_ref, bwd_ref)):
        for block in range(source.shape[0] // LANES):
            turned = source[block * LANES : (block + 1) * LANES, :].T
            out_ref[which, pl.ds(block, LANES, stride=8), :] = turned


def filter_kernel(skip_ref, filt_ref, forward_ref, mix_ref, twiddle_ref, ahead_ref, gain_ref):
    n = LANES
    for c in range(8):
        pair = [filt_ref[which, :, c].reshape(n, n) for which in range(2)]
        spectra = transform(pair, forward_ref, mix_ref, twiddle_ref)
        back_real, back_imag = spectra[n:, :n], -spectra[n:, n:]
        cosine, sine = ahead_ref[0], ahead_ref[1]
        gain_ref[c, 0] = spectra[:n, :n] + (back_real * cosine - back_imag * sine) + skip_ref[c]
        gain_ref[c, 1] = spectra[:n, n:] + (back_real * sine + back_imag * cosine)


def conv_kernel(sig_ref, gain_ref, forward_ref, mix_ref, unmix_ref, backward_ref, twiddle_ref, out_ref):
    n = LANES
    cosine, sine = twiddle_ref[0], twiddle_ref[1]
    for c in range(0, 8, 2):
        pair = [sig_ref[:, c + i].reshape(n, n) for i in range(2)]
        spectra = transform(pair, forward_ref, mix_ref, twiddle_ref)
        rows = []
        for i in range(2):
            real, imag = spectra[i * n : (i + 1) * n, :n], spectra[i * n : (i + 1) * n, n:]
            gain_real, gain_imag = gain_ref[c + i, 0], gain_ref[c + i, 1]
            rows.append(
                jnp.concatenate(
                    [real * gain_real - imag * gain_imag, real * gain_imag + imag * gain_real], axis=1
                )
            )
        parts = right_dot(jnp.concatenate(rows, axis=0), unmix_ref)
        columns = []
        for i in range(2):
            real, imag = parts[i * n : (i + 1) * n, :n], parts[i * n : (i + 1) * n, n:]
            columns.append(
                jnp.concatenate([real * cosine + imag * sine, imag * cosine - real * sine], axis=0)
            )
        times = left_dot(backward_ref[...], jnp.concatenate(columns, axis=1))
        for i in range(2):
            out_ref[:, c + i] = times[:, i * n : (i + 1) * n].reshape(16, 8, n)


def project_kernel(tokens_ref, gain_ref, weight_ref, short_ref, signal_ref, gate_ref, projected_ref):
    count, rows, width = tokens_ref.shape
    weight = jnp.concatenate([weight_ref[j] for j in range(3)], axis=1)
    starts = [0] + [HALO + LANES * i for i in range((rows - HALO) // LANES)]
    for start in starts:
        size = HALO if start == 0 else LANES
        pieces = [tokens_ref[j, start : start + size, :].astype(F32) for j in range(count)]
        total = sum(jnp.sum(piece * piece, axis=1, keepdims=True) for piece in pieces)
        inv_rms = lax.rsqrt(total * (1.0 / (count * width)) + 1e-05)
        normed = jnp.concatenate(
            [(pieces[j] * inv_rms * gain_ref[j : j + 1, :]).astype(BF16) for j in range(count)], axis=1
        )
        projected_ref[start : start + size, :] = dot(normed, weight)
        if start == 0:
            continue
        mixes = []
        for j in range(3):
            columns = slice(j * LANES, (j + 1) * LANES)
            mixes.append(
                sum(
                    short_ref[i, j : j + 1, :] * projected_ref[start - i : start - i + size, columns]
                    for i in range(3)
                )
            )
        block = (start - HALO) // LANES
        signal_ref[pl.ds(block, LANES, stride=8), :] = (mixes[0] * mixes[1]).T
        gate_ref[start - HALO : start - HALO + size, :] = mixes[2]


def gate_kernel(conv_ref, gate_ref, out_ref):
    for block in range(gate_ref.shape[0] // LANES):
        rows = slice(block * LANES, (block + 1) * LANES)
        conv = conv_ref[pl.ds(block, LANES, stride=8), :].T
        out_ref[rows, :] = (gate_ref[rows, :] * conv).astype(BF16)


def output_kernel(index_ref, gated_ref, weight_ref, tokens_ref, out_ref):
    columns = pl.ds(pl.multiple_of(index_ref[0] * LANES, LANES), LANES)
    count, rows, _ = gated_ref.shape
    weight = weight_ref[:, columns]
    for start in range(0, rows, 256):
        gated = jnp.concatenate([gated_ref[j, start : start + 256, :] for j in range(count)], axis=1)
        out_ref[start : start + 256, :] = tokens_ref[start : start + 256, :].astype(F32) + dot(gated, weight)


def local(tokens, norm_gain, in_weight, short_kernel, filter_fwd, filter_bwd, skip_gain, out_weight):
    seq_count = lax.axis_size("seq")
    seq_index = lax.axis_index("seq")
    chan_index = lax.axis_index("chan")
    block_rows, width = tokens.shape
    table = {name: jnp.asarray(value) for name, value in tables().items()}

    halo = lax.ppermute(tokens[block_rows - HALO :], "seq", [(i, i + 1) for i in range(seq_count - 1)])
    gathered = lax.all_gather(jnp.concatenate([halo, tokens], axis=0), "chan", axis=0)
    weights = lax.all_gather(out_weight, "chan", axis=0, tiled=True)

    spread = pl.pallas_call(
        spread_kernel,
        out_shape=jax.ShapeDtypeStruct((2, block_rows, width), F32),
        in_specs=[VMEM] * 2,
        out_specs=VMEM,
        compiler_params=params(),
    )(filter_fwd, filter_bwd)
    filters = lax.all_to_all(spread.reshape(2, seq_count, 8, 8, width), "seq", 1, 1)
    my_skip = lax.dynamic_slice(skip_gain, (seq_index * 8,), (8,))
    gain = pl.pallas_call(
        filter_kernel,
        out_shape=jax.ShapeDtypeStruct((8, 2, LANES, LANES), F32),
        in_specs=[pl.BlockSpec(memory_space=pltpu.SMEM)] + [VMEM] * 5,
        out_specs=VMEM,
        compiler_params=params(),
    )(my_skip, filters, table["forward"], table["mix"], table["twiddle"], table["ahead"])

    signal, gate = pl.pallas_call(
        project_kernel,
        out_shape=(
            jax.ShapeDtypeStruct((block_rows, width), F32),
            jax.ShapeDtypeStruct((block_rows, width), F32),
        ),
        in_specs=[VMEM] * 4,
        out_specs=(VMEM, VMEM),
        scratch_shapes=[pltpu.VMEM((block_rows + HALO, 3 * width), F32)],
        compiler_params=params(),
    )(gathered, norm_gain.reshape(-1, width), in_weight, short_kernel)

    signal = lax.all_to_all(signal.reshape(seq_count, 8, 8, width), "seq", 0, 0)
    conv = pl.pallas_call(
        conv_kernel,
        out_shape=jax.ShapeDtypeStruct((seq_count, 8, 8, width), F32),
        in_specs=[VMEM] * 7,
        out_specs=VMEM,
        compiler_params=params(),
    )(signal, gain, table["forward"], table["mix"], table["unmix"], table["backward"], table["twiddle"])
    conv = lax.all_to_all(conv, "seq", 0, 0)
    gated = pl.pallas_call(
        gate_kernel,
        out_shape=jax.ShapeDtypeStruct((block_rows, width), BF16),
        in_specs=[VMEM] * 2,
        out_specs=VMEM,
        compiler_params=params(),
    )(conv.reshape(block_rows, width), gate)
    all_gated = lax.all_gather(gated, "chan", axis=0)
    return pl.pallas_call(
        output_kernel,
        out_shape=jax.ShapeDtypeStruct((block_rows, width), F32),
        in_specs=[pl.BlockSpec(memory_space=pltpu.SMEM)] + [VMEM] * 3,
        out_specs=VMEM,
        compiler_params=params(),
    )(chan_index.reshape(1), all_gated, weights, tokens)


def solution(mesh):
    return jax.shard_map(
        local,
        mesh=mesh,
        in_specs=(
            P("seq", "chan"),
            P(),
            P(None, None, "chan"),
            P(None, None, "chan"),
            P("seq", "chan"),
            P("seq", "chan"),
            P("chan"),
            P("chan", None),
        ),
        out_specs=P("seq", "chan"),
        check_vma=False,
    )
```

```python
import functools

import jax
import jax.numpy as jnp
import ml_dtypes
import numpy as np
from jax import lax
from jax.experimental import pallas as pl
from jax.experimental.pallas import tpu as pltpu
from jax.sharding import PartitionSpec as P

HALO = 16
PROJECT_FLOPS = 6 * 10**9
LANES = 128
VMEM_LIMIT = 16 * 1024 * 1024
VMEM = pl.BlockSpec(memory_space=pltpu.VMEM)
F32 = jnp.float32
BF16 = jnp.bfloat16


def split_np(table):
    high = table.astype(np.float32).astype(ml_dtypes.bfloat16)
    low = (table - high.astype(np.float64)).astype(np.float32).astype(ml_dtypes.bfloat16)
    return high, low


@functools.cache
def tables():
    n = LANES
    period = 2 * n * n
    k = np.arange(n, dtype=np.float64)
    first = 2 * np.pi * np.outer(k + 0.5, k) / (2 * n)
    forward = np.concatenate([np.cos(first), -np.sin(first)], axis=0)
    backward = np.concatenate([np.cos(first).T, -np.sin(first).T], axis=1) * (2.0 / period)
    second = 2 * np.pi * np.outer(k, k) / n
    cosine, sine = np.cos(second), np.sin(second)
    mix = np.block([[cosine, -sine], [sine, cosine]])
    unmix = np.block([[cosine, sine], [-sine, cosine]])
    turn = 2 * np.pi * np.outer(k + 0.5, k) / period
    twiddle = np.stack([np.cos(turn), -np.sin(turn)]).astype(np.float32)
    step = 2 * np.pi * (k[:, None] + 0.5 + 2 * n * k[None, :]) / period
    ahead = np.stack([np.cos(step), np.sin(step)]).astype(np.float32)
    forward_hi, forward_lo = split_np(forward)
    backward_hi, backward_lo = split_np(backward)
    mix_hi, mix_lo = split_np(mix)
    unmix_hi, unmix_lo = split_np(unmix)
    return {
        "forward": np.concatenate([forward_hi, forward_lo, forward_hi], axis=1),
        "backward": np.concatenate([backward_hi, backward_lo, backward_hi], axis=1),
        "mix": np.concatenate([mix_hi, mix_lo], axis=0),
        "unmix": np.concatenate([unmix_hi, unmix_lo], axis=0),
        "twiddle": twiddle,
        "ahead": ahead,
    }


def halves(value):
    high = value.astype(BF16)
    return high, (value - high.astype(F32)).astype(BF16)


def dot(left, right):
    return jnp.dot(left, right, preferred_element_type=F32)


def left_dot(table, value):
    high, low = halves(value)
    return dot(table, jnp.concatenate([high, high, low], axis=0))


def right_dot(value, table_ref):
    high, low = halves(value)
    depth = value.shape[1]
    table_hi = table_ref[:depth]
    return dot(jnp.concatenate([high, low, high], axis=1), jnp.concatenate([table_hi, table_hi, table_ref[depth:]], axis=0))


def transform(pair, forward_ref, mix_ref, twiddle_ref):
    n = LANES
    parts = left_dot(forward_ref[...], jnp.concatenate(pair, axis=1))
    cosine, sine = twiddle_ref[0], twiddle_ref[1]
    rows = []
    for i in range(2):
        real = parts[:n, i * n : (i + 1) * n]
        imag = parts[n:, i * n : (i + 1) * n]
        rows.append(jnp.concatenate([real * cosine - imag * sine, real * sine + imag * cosine], axis=1))
    return right_dot(jnp.concatenate(rows, axis=0), mix_ref)


def spread_kernel(fwd_ref, bwd_ref, out_ref):
    for which, source in enumerate((fwd_ref, bwd_ref)):
        for block in range(source.shape[0] // LANES):
            turned = source[block * LANES : (block + 1) * LANES, :].T
            for d in range(16):
                out_ref[d, which, pl.ds(block, 8, stride=8), :] = turned[d * 8 : (d + 1) * 8, :]


def filter_kernel(skip_ref, filt_ref, forward_ref, mix_ref, twiddle_ref, ahead_ref, gain_ref):
    n = LANES
    for c in range(8):
        pair = [filt_ref[:, which, c].reshape(n, n) for which in range(2)]
        spectra = transform(pair, forward_ref, mix_ref, twiddle_ref)
        back_real, back_imag = spectra[n:, :n], -spectra[n:, n:]
        cosine, sine = ahead_ref[0], ahead_ref[1]
        gain_ref[c, 0] = spectra[:n, :n] + (back_real * cosine - back_imag * sine) + skip_ref[c]
        gain_ref[c, 1] = spectra[:n, n:] + (back_real * sine + back_imag * cosine)


def conv_kernel(sig_ref, gain_ref, forward_ref, mix_ref, unmix_ref, backward_ref, twiddle_ref, out_ref):
    n = LANES
    cosine, sine = twiddle_ref[0], twiddle_ref[1]
    extra = sig_ref[:, 8]
    before = jnp.concatenate([jnp.zeros((1, 8, n), F32), extra[:-1]], axis=0).reshape(n, n)
    mixes = extra.reshape(n, n) + pltpu.roll(before, n - 4, 1)
    first = (mixes * pltpu.roll(mixes, n - 2, 1)).reshape(16, 8, n)
    at_first = jnp.logical_and(
        lax.broadcasted_iota(jnp.int32, (16, 8, n), 1) == 0, lax.broadcasted_iota(jnp.int32, (16, 8, n), 2) < 2
    )
    for c in range(0, 8, 2):
        pair = [
            jnp.where(at_first, first[:, c + i : c + i + 1, :], sig_ref[:, c + i]).reshape(n, n) for i in range(2)
        ]
        spectra = transform(pair, forward_ref, mix_ref, twiddle_ref)
        rows = []
        for i in range(2):
            real, imag = spectra[i * n : (i + 1) * n, :n], spectra[i * n : (i + 1) * n, n:]
            gain_real, gain_imag = gain_ref[c + i, 0], gain_ref[c + i, 1]
            rows.append(
                jnp.concatenate(
                    [real * gain_real - imag * gain_imag, real * gain_imag + imag * gain_real], axis=1
                )
            )
        parts = right_dot(jnp.concatenate(rows, axis=0), unmix_ref)
        columns = []
        for i in range(2):
            real, imag = parts[i * n : (i + 1) * n, :n], parts[i * n : (i + 1) * n, n:]
            columns.append(
                jnp.concatenate([real * cosine + imag * sine, imag * cosine - real * sine], axis=0)
            )
        times = left_dot(backward_ref[...], jnp.concatenate(columns, axis=1))
        for i in range(2):
            out_ref[:, c + i] = times[:, i * n : (i + 1) * n].reshape(16, 8, n)


def piece_block(j, z, core):
    return (z + 4 - j % 4) % 4 * 2 + (core if j < 4 else 1 - core)


def project_kernel(index_ref, *refs):
    pieces = refs[:8]
    gain_ref, weight_ref, short_ref, message_ref, gate_ref, late_ref, projected_ref, stacked_ref = refs[8:]
    rows, width = pieces[0].shape
    z, core = index_ref[0] // 2, index_ref[0] % 2
    gains = []
    for j in range(8):
        block = piece_block(j, z, core)
        gains.append(gain_ref[pl.ds(block, 1), :])
        source = pl.ds(pl.multiple_of(block * width, width), width)
        for k in range(3):
            stacked_ref[j * width : (j + 1) * width, k * width : (k + 1) * width] = weight_ref[k, source, :]
    projected_ref[:HALO, :] = jnp.zeros((HALO, 3 * width), F32)
    step = 256
    for start in range(0, rows, step):
        parts = [piece[start : start + step, :].astype(F32) for piece in pieces]
        total = sum(part * part for part in parts)
        inv_rms = lax.rsqrt(jnp.sum(total, axis=1, keepdims=True) * (1.0 / (8 * width)) + 1e-05)
        normed = jnp.concatenate([(part * inv_rms * gain).astype(BF16) for part, gain in zip(parts, gains)], axis=1)
        projected_ref[HALO + start : HALO + start + step, :] = dot(normed, stacked_ref[...])
    taps = [[short_ref[i, j : j + 1, :] for j in range(3)] for i in range(3)]
    for block in range(rows // LANES):
        start = block * LANES
        mixes = []
        for j in range(3):
            columns = slice(j * width, (j + 1) * width)
            mixes.append(
                sum(
                    taps[i][j] * projected_ref[HALO + start - i : HALO + start - i + LANES, columns]
                    for i in range(3)
                )
            )
        turned = (mixes[0] * mixes[1]).T
        for d in range(16):
            message_ref[pl.ds(d * 72 + block, 8, stride=8), :] = turned[d * 8 : (d + 1) * 8, :]
        gate_ref[start : start + LANES, :] = mixes[2]
        if block == 0:
            early = [mixes[0][:2], mixes[1][:2]]
    later = []
    for j in range(3):
        columns = slice(j * width, (j + 1) * width)
        last = projected_ref[HALO + rows - 1 : HALO + rows, columns]
        before = projected_ref[HALO + rows - 2 : HALO + rows - 1, columns]
        later.append(jnp.concatenate([taps[1][j] * last + taps[2][j] * before, taps[2][j] * last], axis=0))
    extra = jnp.concatenate(early + later[:2] + [jnp.zeros((LANES - 8, width), F32)], axis=0).T
    for d in range(16):
        message_ref[d * 72 + 64 : d * 72 + 72, :] = extra[d * 8 : (d + 1) * 8, :]
    late_ref[...] = jnp.concatenate([later[2], jnp.zeros((6, width), F32)], axis=0)


def gate_kernel(conv_ref, gate_ref, late_ref, out_ref):
    late = late_ref[...]
    for block in range(gate_ref.shape[0] // LANES):
        rows = slice(block * LANES, (block + 1) * LANES)
        conv = conv_ref[pl.ds(block, LANES, stride=8), :].T
        gate = gate_ref[rows, :]
        if block == 0:
            gate = jnp.concatenate([gate[:8] + late, gate[8:]], axis=0)
        out_ref[rows, :] = (gate * conv).astype(BF16)


def output_kernel(*refs):
    gated, weight_ref, tokens_ref, out_ref = refs[:8], refs[8], refs[9], refs[10]
    rows, width = out_ref.shape
    weight = weight_ref[...]
    step = 256
    for start in range(0, rows, step):
        piece = slice(start, start + step)
        product = dot(jnp.concatenate([ref[piece, :] for ref in gated], axis=1), weight)
        out_ref[piece, :] = tokens_ref[piece, :].astype(F32) + product


def around(value, steps):
    count = lax.axis_size("chan")
    return lax.ppermute(value, "chan", [(i, (i + 2 * steps) % count) for i in range(count)])


def across(value):
    return lax.ppermute(value, "chan", [(i, i ^ 1) for i in range(lax.axis_size("chan"))])


def gather(value):
    mine = [value] + [around(value, steps) for steps in (1, 2, 3)]
    return mine + [across(piece) for piece in mine]


def after(*values):
    return lax.optimization_barrier(values)


def call(kernel, shapes, *operands, scalars=0, scratch=(), cost=None):
    smem = pl.BlockSpec(memory_space=pltpu.SMEM)
    return pl.pallas_call(
        kernel,
        out_shape=shapes,
        in_specs=[smem] * scalars + [VMEM] * (len(operands) - scalars),
        out_specs=jax.tree.map(lambda _: VMEM, shapes),
        scratch_shapes=scratch,
        cost_estimate=cost,
        compiler_params=pltpu.CompilerParams(vmem_limit_bytes=VMEM_LIMIT),
    )(*operands)


def local(tokens, norm_gain, in_weight, short_kernel, filter_fwd, filter_bwd, skip_gain, out_weight):
    seq_count = lax.axis_size("seq")
    seq_index = lax.axis_index("seq")
    chan_index = lax.axis_index("chan").reshape(1)
    rows, width = tokens.shape
    table = {name: jnp.asarray(value) for name, value in tables().items()}
    shape = jax.ShapeDtypeStruct

    pieces = [tokens] + [around(tokens, steps) for steps in (1, 2, 3)]
    spread = call(spread_kernel, shape((seq_count, 2, 64, width), F32), filter_fwd, filter_bwd)
    pieces = pieces + [across(piece) for piece in pieces]
    filters = lax.all_to_all(spread, "seq", 0, 0).reshape(seq_count, 2, 8, 8, width)
    my_skip = lax.dynamic_slice(skip_gain, (seq_index * 8,), (8,))
    gain = call(
        filter_kernel,
        shape((8, 2, LANES, LANES), F32),
        my_skip,
        filters,
        table["forward"],
        table["mix"],
        table["twiddle"],
        table["ahead"],
        scalars=1,
    )

    message, gate, late = call(
        project_kernel,
        (shape((seq_count * 72, width), F32), shape((rows, width), F32), shape((8, width), F32)),
        chan_index,
        *pieces,
        norm_gain.reshape(-1, width),
        in_weight,
        short_kernel,
        scalars=1,
        scratch=[pltpu.VMEM((rows + HALO, 3 * width), F32), pltpu.VMEM((8 * width, 3 * width), BF16)],
        cost=pl.CostEstimate(flops=PROJECT_FLOPS, bytes_accessed=1, transcendentals=0),
    )
    message, filters = after(message, filters)
    signal = lax.all_to_all(message.reshape(seq_count, 9, 8, width), "seq", 0, 0)
    late = lax.ppermute(late, "seq", [(i, i + 1) for i in range(seq_count - 1)])
    z = chan_index[0] // 2
    column = [lax.dynamic_slice(out_weight, (0, (z + steps) % 4 * 2 * width), (width, 2 * width)) for steps in range(4)]
    column = [column[0]] + [around(column[steps], steps) for steps in (1, 2, 3)]
    signal, *column = after(signal, *column)
    conv = call(
        conv_kernel,
        shape((seq_count, 8, 8, width), F32),
        signal,
        gain,
        table["forward"],
        table["mix"],
        table["unmix"],
        table["backward"],
        table["twiddle"],
    )
    conv = lax.all_to_all(conv, "seq", 0, 0)
    column = jnp.concatenate(column, axis=0)
    core = chan_index[0] % 2
    mine, theirs = [lax.dynamic_slice(column, (0, c * width), (4 * width, width)) for c in (core, 1 - core)]
    conv, theirs = after(conv, across(theirs))
    weights = jnp.concatenate([mine, theirs], axis=0)
    gated = call(gate_kernel, shape((rows, width), BF16), conv.reshape(rows, width), gate, late)
    return call(output_kernel, shape((rows, width), F32), *gather(gated), weights, tokens)


def solution(mesh):
    return jax.shard_map(
        local,
        mesh=mesh,
        in_specs=(
            P("seq", "chan"),
            P(),
            P(None, None, "chan"),
            P(None, None, "chan"),
            P("seq", "chan"),
            P("seq", "chan"),
            P("chan"),
            P("chan", None),
        ),
        out_specs=P("seq", "chan"),
        check_vma=False,
    )
```

```python
import functools

import jax
import jax.numpy as jnp
import ml_dtypes
import numpy as np
from jax import lax
from jax.experimental import pallas as pl
from jax.experimental.pallas import tpu as pltpu
from jax.sharding import PartitionSpec as P

HALO = 16
PROJECT_FLOPS = 1.5e9
LANES = 128
VMEM_LIMIT = 16 * 1024 * 1024
VMEM = pl.BlockSpec(memory_space=pltpu.VMEM)
F32 = jnp.float32
BF16 = jnp.bfloat16


def split_np(table):
    high = table.astype(np.float32).astype(ml_dtypes.bfloat16)
    low = (table - high.astype(np.float64)).astype(np.float32).astype(ml_dtypes.bfloat16)
    return high, low


@functools.cache
def tables():
    n = LANES
    period = 2 * n * n
    k = np.arange(n, dtype=np.float64)
    first = 2 * np.pi * np.outer(k + 0.5, k) / (2 * n)
    forward = np.concatenate([np.cos(first), -np.sin(first)], axis=0)
    second = 2 * np.pi * np.outer(k, k) / n
    cosine, sine = np.cos(second), np.sin(second)
    mix = np.block([[cosine, -sine], [sine, cosine]])
    turn = 2 * np.pi * np.outer(k + 0.5, k) / period
    twiddle = np.stack([np.cos(turn), -np.sin(turn)]).astype(np.float32)
    forward_hi, forward_lo = split_np(forward)
    mix_hi, mix_lo = split_np(mix)
    return {
        "forward": np.concatenate([forward_hi, forward_lo], axis=1),
        "mix": np.concatenate([mix_hi, mix_lo], axis=0),
        "twiddle": twiddle,
    }


def halves(value):
    high = value.astype(BF16)
    return high, (value - high.astype(F32)).astype(BF16)


def dot(left, right):
    return jnp.dot(left, right, preferred_element_type=F32)


def left_dot(table_ref, value):
    high, low = halves(value)
    table_hi, table_lo = [table_ref[:, i * LANES : (i + 1) * LANES].T for i in range(2)]
    return dot(
        jnp.concatenate([table_hi, table_lo, table_hi], axis=1), jnp.concatenate([high, high, low], axis=0)
    )


def right_dot(value, table_ref, transposed=False):
    high, low = halves(value)
    depth = value.shape[1]
    table_hi, table_lo = table_ref[:depth], table_ref[depth:]
    left = jnp.concatenate([high, low, high], axis=1)
    if transposed:
        right = jnp.concatenate([table_hi, table_hi, table_lo], axis=1)
        return lax.dot_general(left, right, (((1,), (1,)), ((), ())), preferred_element_type=F32)
    return dot(left, jnp.concatenate([table_hi, table_hi, table_lo], axis=0))


def transform(sequences, forward_ref, mix_ref, twiddle_ref):
    n = LANES
    value = jnp.concatenate(sequences, axis=1)
    parts = dot(forward_ref[...], jnp.concatenate([value, value], axis=0))
    cosine, sine = twiddle_ref[0], twiddle_ref[1]
    rows = []
    for i in range(len(sequences)):
        real = parts[:n, i * n : (i + 1) * n]
        imag = parts[n:, i * n : (i + 1) * n]
        rows.append(jnp.concatenate([real * cosine - imag * sine, real * sine + imag * cosine], axis=1))
    return right_dot(jnp.concatenate(rows, axis=0), mix_ref)


def spread_kernel(index_ref, fwd_ref, bwd_ref, weight_ref, out_ref, *refs):
    columns_refs, turned_ref = refs[:3], refs[3]
    z = index_ref[0] // 2
    for steps, columns_ref in enumerate(columns_refs):
        start = pl.multiple_of((z + steps + 1) % 4 * 2 * LANES, 2 * LANES)
        columns_ref[...] = weight_ref[:, pl.ds(start, 2 * LANES)]
    for which, source in enumerate((fwd_ref, bwd_ref)):
        for block in range(source.shape[0] // LANES):
            turned_ref[pl.ds(block, LANES, stride=8), :] = source[block * LANES : (block + 1) * LANES, :].T
        out_ref[:, which * 64 : (which + 1) * 64, :] = turned_ref[...].reshape(16, 64, LANES).astype(BF16)


def channel_pair(ref, start):
    both = ref[:, start : start + 16, :].astype(F32)
    return both[:, :8], both[:, 8:]


def filter_kernel(filt_ref, forward_ref, mix_ref, twiddle_ref, gain_ref):
    n = LANES
    row = mix_ref[:8, :].astype(F32) + mix_ref[2 * n : 2 * n + 8, :].astype(F32)
    row_real, row_imag = row[1:2, :n], -row[1:2, n:]
    column_real, column_imag = twiddle_ref[0, :, 1:2], -twiddle_ref[1, :, 1:2]
    cosine = column_real * row_real - column_imag * row_imag
    sine = column_real * row_imag + column_imag * row_real
    for c in range(0, 8, 2):
        forth, back = [channel_pair(filt_ref, 64 * which + 8 * c) for which in range(2)]
        spectra = transform(
            [part.reshape(n, n).astype(BF16) for part in forth + back], forward_ref, mix_ref, twiddle_ref
        )
        for i in range(2):
            forth_rows = slice(i * n, (i + 1) * n)
            back_rows = slice((2 + i) * n, (3 + i) * n)
            back_real, back_imag = spectra[back_rows, :n], -spectra[back_rows, n:]
            gain_ref[c + i, 0] = spectra[forth_rows, :n] + (back_real * cosine - back_imag * sine)
            gain_ref[c + i, 1] = spectra[forth_rows, n:] + (back_real * sine + back_imag * cosine)


def conv_kernel(sig_ref, gain_ref, forward_ref, mix_ref, twiddle_ref, out_ref):
    n = LANES
    extra_high, extra_low = channel_pair(sig_ref, 64)
    extra = extra_high + extra_low
    before = jnp.concatenate([jnp.zeros((1, 8, n), F32), extra[:-1]], axis=0)
    high = before.astype(BF16).astype(F32)
    out_ref[:, 64:, :] = jnp.concatenate([high, before - high], axis=1).astype(BF16)
    before = before.reshape(n, n)
    mixes = extra.reshape(n, n) + pltpu.roll(before, n - 4, 1)
    first = (mixes * pltpu.roll(mixes, n - 2, 1)).reshape(16, 8, n)
    at_first = jnp.logical_and(
        lax.broadcasted_iota(jnp.int32, (16, 8, n), 1) == 0, lax.broadcasted_iota(jnp.int32, (16, 8, n), 2) < 2
    )
    cosine, sine = twiddle_ref[0], twiddle_ref[1]
    for c in range(0, 8, 2):
        pair = [
            jnp.where(at_first, first[:, c + i : c + i + 1, :], part).reshape(n, n).astype(BF16)
            for i, part in enumerate(channel_pair(sig_ref, 8 * c))
        ]
        spectra = transform(pair, forward_ref, mix_ref, twiddle_ref)
        rows = []
        for i in range(2):
            real, imag = spectra[i * n : (i + 1) * n, :n], spectra[i * n : (i + 1) * n, n:]
            gain_real = gain_ref[c + i, 0] + extra[0, c + i : c + i + 1, 10:11]
            gain_imag = gain_ref[c + i, 1]
            rows.append(
                jnp.concatenate(
                    [real * gain_real - imag * gain_imag, real * gain_imag + imag * gain_real], axis=1
                )
            )
        parts = right_dot(jnp.concatenate(rows, axis=0), mix_ref, transposed=True)
        columns = []
        for i in range(2):
            real, imag = parts[i * n : (i + 1) * n, :n], parts[i * n : (i + 1) * n, n:]
            columns.append(
                jnp.concatenate([real * cosine + imag * sine, imag * cosine - real * sine], axis=0)
            )
        times = left_dot(forward_ref, jnp.concatenate(columns, axis=1)) * (1.0 / (n * n))
        blocks = [times[:, i * n : (i + 1) * n].reshape(16, 8, n) for i in range(2)]
        out_ref[:, 8 * c : 8 * c + 16, :] = jnp.concatenate(blocks, axis=1).astype(BF16)


def piece_block(j, z, core):
    return (z + 4 - j % 4) % 4 * 2 + (core if j < 4 else 1 - core)


def project_kernel(index_ref, *refs):
    pieces, refs = refs[:8], refs[8:]
    gain_ref, weight_ref, short_ref, skip_ref, message_ref, gate_ref, projected_ref, stacked_ref, turned_ref = refs
    rows, width = pieces[0].shape
    z, core = index_ref[0] // 2, index_ref[0] % 2
    gains = []
    for j in range(8):
        block = piece_block(j, z, core)
        gains.append(gain_ref[pl.ds(block, 1), :])
        source = pl.ds(pl.multiple_of(block * width, width), width)
        for k in range(3):
            stacked_ref[j * width : (j + 1) * width, k * width : (k + 1) * width] = weight_ref[k, source, :]
    projected_ref[:HALO, :] = jnp.zeros((HALO, 3 * width), F32)
    step = 256
    for start in range(0, rows, step):
        parts = [piece[start : start + step, :].astype(F32) for piece in pieces]
        total = sum(part * part for part in parts)
        inv_rms = lax.rsqrt(jnp.sum(total, axis=1, keepdims=True) * (1.0 / (8 * width)) + 1e-05)
        normed = jnp.concatenate([(part * inv_rms * gain).astype(BF16) for part, gain in zip(parts, gains)], axis=1)
        projected_ref[HALO + start : HALO + start + step, :] = dot(normed, stacked_ref[...])
    taps = [[short_ref[i, j : j + 1, :] for j in range(3)] for i in range(3)]
    for block in range(rows // LANES):
        start = block * LANES
        mixes = []
        for j in range(3):
            columns = slice(j * width, (j + 1) * width)
            mixes.append(
                sum(
                    taps[i][j] * projected_ref[HALO + start - i : HALO + start - i + LANES, columns]
                    for i in range(3)
                )
            )
        turned_ref[pl.ds(block, LANES, stride=8), :] = (mixes[0] * mixes[1]).T
        gate_ref[start : start + LANES, :] = mixes[2]
        if block == 0:
            early = [mixes[0][:2], mixes[1][:2]]
    later = []
    for j in range(3):
        columns = slice(j * width, (j + 1) * width)
        last = projected_ref[HALO + rows - 1 : HALO + rows, columns]
        before = projected_ref[HALO + rows - 2 : HALO + rows - 1, columns]
        later.append(jnp.concatenate([taps[1][j] * last + taps[2][j] * before, taps[2][j] * last], axis=0))
    extra = jnp.concatenate(early + later + [skip_ref[...], jnp.zeros((LANES - 11, width), F32)], axis=0).T
    high = extra.astype(BF16).astype(F32)
    message_ref[:, :64, :] = turned_ref[...].reshape(16, 64, LANES).astype(BF16)
    message_ref[:, 64:, :] = jnp.concatenate(
        [high.reshape(16, 8, LANES), (extra - high).reshape(16, 8, LANES)], axis=1
    ).astype(BF16)


def gate_kernel(index_ref, conv_ref, gate_ref, weight_ref, *refs):
    columns_refs, (out_ref, mine_ref, theirs_ref, turned_ref) = refs[:3], refs[3:]
    z, core = index_ref[0] // 2, index_ref[0] % 2
    for k in range(4):
        for ref, c in ((mine_ref, core), (theirs_ref, 1 - core)):
            start = c * LANES if k else (2 * z + c) * LANES
            source = columns_refs[k - 1] if k else weight_ref
            ref[k * LANES : (k + 1) * LANES, :] = source[:, pl.ds(pl.multiple_of(start, LANES), LANES)]
    turned_ref[...] = conv_ref[:, :64, :].astype(F32).reshape(turned_ref.shape)
    extra_high, extra_low = channel_pair(conv_ref, 64)
    late = (extra_high + extra_low).reshape(LANES, LANES).T[8:10]
    for block in range(gate_ref.shape[0] // LANES):
        rows = slice(block * LANES, (block + 1) * LANES)
        conv = turned_ref[pl.ds(block, LANES, stride=8), :].T
        gate = gate_ref[rows, :]
        if block == 0:
            gate = jnp.concatenate([gate[:2] + late, gate[2:]], axis=0)
        out_ref[rows, :] = (gate * conv).astype(BF16)


def output_kernel(*refs):
    gated, mine_ref, theirs_ref, tokens_ref, out_ref = refs[:8], *refs[8:]
    weight = jnp.concatenate([mine_ref[...], theirs_ref[...]], axis=0)
    step = 256
    for start in range(0, out_ref.shape[0], step):
        piece = slice(start, start + step)
        product = dot(jnp.concatenate([ref[piece, :] for ref in gated], axis=1), weight)
        out_ref[piece, :] = tokens_ref[piece, :].astype(F32) + product


def around(value, steps):
    count = lax.axis_size("chan")
    return lax.ppermute(value, "chan", [(i, (i + 2 * steps) % count) for i in range(count)])


def across(value):
    return lax.ppermute(value, "chan", [(i, i ^ 1) for i in range(lax.axis_size("chan"))])


def gather(value):
    mine = [value] + [around(value, steps) for steps in (1, 2, 3)]
    return mine + [across(piece) for piece in mine]


def after(*values):
    return lax.optimization_barrier(values)


def call(kernel, shapes, *operands, scalars=0, scratch=(), cost=None):
    smem = pl.BlockSpec(memory_space=pltpu.SMEM)
    return pl.pallas_call(
        kernel,
        out_shape=shapes,
        in_specs=[smem] * scalars + [VMEM] * (len(operands) - scalars),
        out_specs=jax.tree.map(lambda _: VMEM, shapes),
        scratch_shapes=scratch,
        cost_estimate=cost,
        compiler_params=pltpu.CompilerParams(vmem_limit_bytes=VMEM_LIMIT),
    )(*operands)


def local(tokens, norm_gain, in_weight, short_kernel, filter_fwd, filter_bwd, skip_gain, out_weight):
    seq_count = lax.axis_size("seq")
    chan_index = lax.axis_index("chan").reshape(1)
    rows, width = tokens.shape
    table = {name: jnp.asarray(value) for name, value in tables().items()}
    shape = jax.ShapeDtypeStruct
    turned = pltpu.VMEM((rows, width), F32)

    pieces = [tokens] + [around(tokens, steps) for steps in (1, 2, 3)]
    spread, *columns = call(
        spread_kernel,
        [shape((seq_count, 128, width), BF16)] + [shape((width, 2 * width), BF16)] * 3,
        chan_index,
        filter_fwd,
        filter_bwd,
        out_weight,
        scalars=1,
        scratch=[turned],
    )
    pieces = pieces + [across(piece) for piece in pieces]
    filters = lax.all_to_all(spread, "seq", 0, 0)
    shared = [table[name] for name in ("forward", "mix", "twiddle")]
    gain = call(filter_kernel, shape((8, 2, LANES, LANES), F32), filters, *shared)

    message, gate = call(
        project_kernel,
        [shape((seq_count, 80, width), BF16), shape((rows, width), F32)],
        chan_index,
        *pieces,
        norm_gain.reshape(-1, width),
        in_weight,
        short_kernel,
        skip_gain.reshape(1, width),
        scalars=1,
        scratch=[
            pltpu.VMEM((rows + HALO, 3 * width), F32),
            pltpu.VMEM((8 * width, 3 * width), BF16),
            turned,
        ],
        cost=pl.CostEstimate(flops=int(PROJECT_FLOPS), bytes_accessed=1, transcendentals=0),
    )
    message, filters = after(message, filters)
    signal = lax.all_to_all(message, "seq", 0, 0)
    conv = call(conv_kernel, shape((seq_count, 80, width), BF16), signal, gain, *shared)
    conv, *columns = after(conv, *columns)
    conv = lax.all_to_all(conv, "seq", 0, 0)
    columns = [around(column, steps) for column, steps in zip(columns, (1, 2, 3))]
    conv, *columns = after(conv, *columns)
    gated, mine, theirs = call(
        gate_kernel,
        [shape((rows, width), BF16)] + [shape((4 * width, width), BF16)] * 2,
        chan_index,
        conv,
        gate,
        out_weight,
        *columns,
        scalars=1,
        scratch=[turned],
    )
    return call(output_kernel, shape((rows, width), F32), *gather(gated), mine, across(theirs), tokens)


def solution(mesh):
    return jax.shard_map(
        local,
        mesh=mesh,
        in_specs=(
            P("seq", "chan"),
            P(),
            P(None, None, "chan"),
            P(None, None, "chan"),
            P("seq", "chan"),
            P("seq", "chan"),
            P("chan"),
            P("chan", None),
        ),
        out_specs=P("seq", "chan"),
        check_vma=False,
    )
```

```python
import functools

import jax
import jax.numpy as jnp
import ml_dtypes
import numpy as np
from jax import lax
from jax.experimental import pallas as pl
from jax.experimental.pallas import tpu as pltpu
from jax.sharding import PartitionSpec as P

HALO = 16
PROJECT_FLOPS = 1.5e9
LANES = 128
VMEM_LIMIT = 16 * 1024 * 1024
VMEM = pl.BlockSpec(memory_space=pltpu.VMEM)
F32 = jnp.float32
BF16 = jnp.bfloat16


def split_np(table):
    high = table.astype(np.float32).astype(ml_dtypes.bfloat16)
    low = (table - high.astype(np.float64)).astype(np.float32).astype(ml_dtypes.bfloat16)
    return high, low


@functools.cache
def tables():
    n = LANES
    period = 2 * n * n
    k = np.arange(n, dtype=np.float64)
    first = 2 * np.pi * np.outer(k + 0.5, k) / (2 * n)
    forward = np.concatenate([np.cos(first), -np.sin(first)], axis=0)
    second = 2 * np.pi * np.outer(k, k) / n
    cosine, sine = np.cos(second), np.sin(second)
    mix = np.block([[cosine, -sine], [sine, cosine]])
    turn = 2 * np.pi * np.outer(k + 0.5, k) / period
    twiddle = np.stack([np.cos(turn), -np.sin(turn)]).astype(np.float32)
    forward_hi, forward_lo = split_np(forward)
    mix_hi, mix_lo = split_np(mix)
    return {
        "forward": np.concatenate([forward_hi, forward_lo], axis=1),
        "mix": np.concatenate([mix_hi, mix_lo], axis=0),
        "twiddle": twiddle,
    }


def halves(value):
    high = value.astype(BF16)
    return high, (value - high.astype(F32)).astype(BF16)


def dot(left, right):
    return jnp.dot(left, right, preferred_element_type=F32)


def left_dot(table_ref, value):
    high, low = halves(value)
    depth = value.shape[0]
    table_hi, table_lo = table_ref[:, :depth], table_ref[:, depth:]
    return dot(jnp.concatenate([table_hi, table_lo, table_hi], axis=1), jnp.concatenate([high, high, low], axis=0))


def right_dot(value, table_ref):
    high, low = halves(value)
    depth = value.shape[1]
    table_hi, table_lo = table_ref[:depth], table_ref[depth:]
    return dot(jnp.concatenate([high, low, high], axis=1), jnp.concatenate([table_hi, table_hi, table_lo], axis=0))


def transform(sequences, forward_ref, mix_ref, twiddle_ref):
    n = LANES
    value = jnp.concatenate(sequences, axis=1)
    parts = dot(forward_ref[...], jnp.concatenate([value, value], axis=0))
    cosine, sine = twiddle_ref[0], twiddle_ref[1]
    rows = []
    for i in range(len(sequences)):
        real = parts[:n, i * n : (i + 1) * n]
        imag = parts[n:, i * n : (i + 1) * n]
        rows.append(jnp.concatenate([real * cosine - imag * sine, real * sine + imag * cosine], axis=1))
    return right_dot(jnp.concatenate(rows, axis=0), mix_ref)


def fetch(pairs, sems):
    copies = [pltpu.make_async_copy(source, target, sems.at[i]) for i, (source, target) in enumerate(pairs)]
    for copy in copies:
        copy.start()
    return copies


def spread_kernel(index_ref, fwd_ref, bwd_ref, weight_ref, out_ref, *refs):
    columns_refs, (held_ref, turned_ref, sems, column_sems) = refs[:3], refs[3:]
    step = 2 * LANES
    places = [(which, start) for which in range(2) for start in range(0, fwd_ref.shape[0], step)]
    copies = fetch(
        [
            ((fwd_ref, bwd_ref)[which].at[pl.ds(start, step), :], held_ref.at[which, pl.ds(start, step), :])
            for which, start in places
        ],
        sems,
    )
    z = index_ref[0] // 2
    columns = fetch(
        [
            (weight_ref.at[:, pl.ds(pl.multiple_of((z + steps) % 4 * 2 * LANES, 2 * LANES), 2 * LANES)], columns_ref)
            for steps, columns_ref in zip((1, 2, 3), columns_refs)
        ],
        column_sems,
    )
    for copy, (which, start) in zip(copies, places):
        copy.wait()
        for block in range(start // LANES, (start + step) // LANES):
            turned = held_ref[which, block * LANES : (block + 1) * LANES, :].T
            turned_ref[which, pl.ds(block, LANES, stride=8), :] = turned
        if start + step == fwd_ref.shape[0]:
            out_ref[:, which * 64 : (which + 1) * 64, :] = turned_ref[which].reshape(16, 64, LANES).astype(BF16)
    for copy in columns:
        copy.wait()


def channel_pair(ref, start):
    both = ref[:, start : start + 16, :].astype(F32)
    return both[:, :8], both[:, 8:]


def filter_kernel(index_ref, skip_ref, filt_ref, forward_ref, mix_ref, twiddle_ref, gain_ref, backward_ref):
    n = LANES
    first_channel = index_ref[0] * 8
    for half in range(2):
        backward_ref[:, 2 * n * half : 2 * n * (half + 1)] = forward_ref[:, n * half : n * (half + 1)].astype(F32).T.astype(BF16)
    row = mix_ref[:8, :].astype(F32) + mix_ref[2 * n : 2 * n + 8, :].astype(F32)
    row_real, row_imag = row[1:2, :n], -row[1:2, n:]
    column_real, column_imag = twiddle_ref[0, :, 1:2], -twiddle_ref[1, :, 1:2]
    cosine = column_real * row_real - column_imag * row_imag
    sine = column_real * row_imag + column_imag * row_real
    for c in range(0, 8, 2):
        forth, back = [channel_pair(filt_ref, 64 * which + 8 * c) for which in range(2)]
        spectra = transform(
            [part.reshape(n, n).astype(BF16) for part in forth + back], forward_ref, mix_ref, twiddle_ref
        )
        for i in range(2):
            forth_rows = slice(i * n, (i + 1) * n)
            back_rows = slice((2 + i) * n, (3 + i) * n)
            back_real, back_imag = spectra[back_rows, :n], -spectra[back_rows, n:]
            gain_ref[c + i, 0] = spectra[forth_rows, :n] + (back_real * cosine - back_imag * sine) + skip_ref[first_channel + c + i]
            gain_ref[c + i, 1] = spectra[forth_rows, n:] + (back_real * sine + back_imag * cosine)


def conv_kernel(sig_ref, gain_ref, forward_ref, mix_ref, twiddle_ref, backward_ref, out_ref):
    n = LANES
    extra_high, extra_low = channel_pair(sig_ref, 64)
    extra = extra_high + extra_low
    before = jnp.concatenate([jnp.zeros((1, 8, n), F32), extra[:-1]], axis=0)
    high = before.astype(BF16).astype(F32)
    out_ref[:, 64:, :] = jnp.concatenate([high, before - high], axis=1).astype(BF16)
    before = before.reshape(n, n)
    mixes = extra.reshape(n, n) + pltpu.roll(before, n - 4, 1)
    first = (mixes * pltpu.roll(mixes, n - 2, 1)).reshape(16, 8, n)
    at_first = jnp.logical_and(
        lax.broadcasted_iota(jnp.int32, (16, 8, n), 1) == 0, lax.broadcasted_iota(jnp.int32, (16, 8, n), 2) < 2
    )
    cosine, sine = twiddle_ref[0], twiddle_ref[1]
    sequences = []
    for c in range(0, 8, 2):
        for i, part in enumerate(channel_pair(sig_ref, 8 * c)):
            sequences.append(jnp.where(at_first, first[:, c + i : c + i + 1, :], part).reshape(n, n).astype(BF16))
    spectra = transform(sequences, forward_ref, mix_ref, twiddle_ref)
    rows = []
    for c in range(8):
        real, imag = spectra[c * n : (c + 1) * n, :n], spectra[c * n : (c + 1) * n, n:]
        gain_real, gain_imag = gain_ref[c, 0], gain_ref[c, 1]
        rows.append(
            jnp.concatenate([real * gain_real - imag * gain_imag, -(real * gain_imag + imag * gain_real)], axis=1)
        )
    parts = right_dot(jnp.concatenate(rows, axis=0), mix_ref)
    columns = []
    for c in range(8):
        real, imag = parts[c * n : (c + 1) * n, :n], parts[c * n : (c + 1) * n, n:]
        columns.append(jnp.concatenate([real * cosine - imag * sine, -(real * sine + imag * cosine)], axis=0))
    times = left_dot(backward_ref, jnp.concatenate(columns, axis=1)) * (1.0 / (n * n))
    blocks = [times[:, c * n : (c + 1) * n].reshape(16, 8, n) for c in range(8)]
    out_ref[:, :64, :] = jnp.concatenate(blocks, axis=1).astype(BF16)


def piece_block(j, z, core):
    return (z + 4 - j % 4) % 4 * 2 + (core if j < 4 else 1 - core)


def project_kernel(index_ref, *refs):
    pieces, refs = refs[:8], refs[8:]
    gain_ref, weight_ref, short_ref, message_ref, gate_ref, projected_ref, stacked_ref, turned_ref = refs
    rows, width = pieces[0].shape
    z, core = index_ref[0] // 2, index_ref[0] % 2
    gains = []
    for j in range(8):
        block = piece_block(j, z, core)
        gains.append(gain_ref[pl.ds(block, 1), :])
        source = pl.ds(pl.multiple_of(block * width, width), width)
        for k in range(3):
            stacked_ref[j * width : (j + 1) * width, k * width : (k + 1) * width] = weight_ref[k, source, :]
    projected_ref[:HALO, :] = jnp.zeros((HALO, 3 * width), F32)
    step = 512
    for start in range(0, rows, step):
        parts = [piece[start : start + step, :].astype(F32) for piece in pieces]
        total = sum(part * part for part in parts)
        inv_rms = lax.rsqrt(jnp.sum(total, axis=1, keepdims=True) * (1.0 / (8 * width)) + 1e-05)
        normed = jnp.concatenate([(part * inv_rms * gain).astype(BF16) for part, gain in zip(parts, gains)], axis=1)
        projected_ref[HALO + start : HALO + start + step, :] = dot(normed, stacked_ref[...])
    taps = [[short_ref[i, j : j + 1, :] for j in range(3)] for i in range(3)]
    for block in range(rows // LANES):
        start = block * LANES
        mixes = []
        for j in range(3):
            columns = slice(j * width, (j + 1) * width)
            mixes.append(
                sum(
                    taps[i][j] * projected_ref[HALO + start - i : HALO + start - i + LANES, columns]
                    for i in range(3)
                )
            )
        turned_ref[pl.ds(block, LANES, stride=8), :] = (mixes[0] * mixes[1]).T
        gate_ref[start : start + LANES, :] = mixes[2]
        if block == 0:
            early = [mixes[0][:2], mixes[1][:2]]
    later = []
    for j in range(3):
        columns = slice(j * width, (j + 1) * width)
        last = projected_ref[HALO + rows - 1 : HALO + rows, columns]
        before = projected_ref[HALO + rows - 2 : HALO + rows - 1, columns]
        later.append(jnp.concatenate([taps[1][j] * last + taps[2][j] * before, taps[2][j] * last], axis=0))
    extra = jnp.concatenate(early + later + [jnp.zeros((LANES - 10, width), F32)], axis=0).T
    high = extra.astype(BF16).astype(F32)
    message_ref[:, :64, :] = turned_ref[...].reshape(16, 64, LANES).astype(BF16)
    message_ref[:, 64:, :] = jnp.concatenate(
        [high.reshape(16, 8, LANES), (extra - high).reshape(16, 8, LANES)], axis=1
    ).astype(BF16)


def gate_kernel(index_ref, conv_ref, gate_ref, weight_ref, *refs):
    columns_refs, (out_ref, mine_ref, theirs_ref, turned_ref) = refs[:3], refs[3:]
    z, core = index_ref[0] // 2, index_ref[0] % 2
    for k in range(4):
        for ref, c in ((mine_ref, core), (theirs_ref, 1 - core)):
            start = c * LANES if k else (2 * z + c) * LANES
            source = columns_refs[k - 1] if k else weight_ref
            ref[k * LANES : (k + 1) * LANES, :] = source[:, pl.ds(pl.multiple_of(start, LANES), LANES)]
    turned_ref[...] = conv_ref[:, :64, :].astype(F32).reshape(turned_ref.shape)
    extra_high, extra_low = channel_pair(conv_ref, 64)
    late = (extra_high + extra_low).reshape(LANES, LANES).T[8:10]
    for block in range(gate_ref.shape[0] // LANES):
        rows = slice(block * LANES, (block + 1) * LANES)
        conv = turned_ref[pl.ds(block, LANES, stride=8), :].T
        gate = gate_ref[rows, :]
        if block == 0:
            gate = jnp.concatenate([gate[:2] + late, gate[2:]], axis=0)
        out_ref[rows, :] = (gate * conv).astype(BF16)


def output_kernel(*refs):
    gated, mine_ref, theirs_ref, tokens_ref, out_ref = refs[:8], *refs[8:]
    weight = jnp.concatenate([mine_ref[...], theirs_ref[...]], axis=0)
    step = 256
    for start in range(0, out_ref.shape[0], step):
        piece = slice(start, start + step)
        product = dot(jnp.concatenate([ref[piece, :] for ref in gated], axis=1), weight)
        out_ref[piece, :] = tokens_ref[piece, :].astype(F32) + product


def around(value, steps):
    count = lax.axis_size("chan")
    return lax.ppermute(value, "chan", [(i, (i + 2 * steps) % count) for i in range(count)])


def across(value):
    return lax.ppermute(value, "chan", [(i, i ^ 1) for i in range(lax.axis_size("chan"))])


def gather(value):
    mine = [value] + [around(value, steps) for steps in (1, 2, 3)]
    return mine + [across(piece) for piece in mine]


def after(*values):
    return lax.optimization_barrier(values)


def call(kernel, shapes, *operands, scalars=0, outside=(), scratch=(), cost=None):
    spaces = [pltpu.SMEM if i < scalars else pltpu.HBM if i in outside else pltpu.VMEM for i in range(len(operands))]
    operands = [
        pltpu.with_memory_space_constraint(operand, space) if space is pltpu.HBM else operand
        for operand, space in zip(operands, spaces)
    ]
    return pl.pallas_call(
        kernel,
        out_shape=shapes,
        in_specs=[pl.BlockSpec(memory_space=space) for space in spaces],
        out_specs=jax.tree.map(lambda _: VMEM, shapes),
        scratch_shapes=scratch,
        cost_estimate=cost,
        compiler_params=pltpu.CompilerParams(vmem_limit_bytes=VMEM_LIMIT),
    )(*operands)


def local(tokens, norm_gain, in_weight, short_kernel, filter_fwd, filter_bwd, skip_gain, out_weight):
    seq_count = lax.axis_size("seq")
    chan_index = lax.axis_index("chan").reshape(1)
    rows, width = tokens.shape
    shape = jax.ShapeDtypeStruct
    turned = pltpu.VMEM((rows, width), F32)

    spread, *columns = call(
        spread_kernel,
        [shape((seq_count, 128, width), BF16)] + [shape((width, 2 * width), BF16)] * 3,
        chan_index,
        filter_fwd,
        filter_bwd,
        out_weight,
        scalars=1,
        outside=(1, 2, 3),
        scratch=[pltpu.VMEM((2, rows, width), F32)] * 2
        + [pltpu.SemaphoreType.DMA((8,)), pltpu.SemaphoreType.DMA((3,))],
    )
    pieces = [tokens] + [around(tokens, steps) for steps in (1, 2, 3)]
    pieces = pieces + [across(piece) for piece in pieces]
    filters = lax.all_to_all(spread, "seq", 0, 0)
    forward, mix, twiddle = [jnp.asarray(tables()[name]) for name in ("forward", "mix", "twiddle")]
    gain, backward = call(
        filter_kernel,
        [shape((8, 2, LANES, LANES), F32), shape((LANES, 4 * LANES), BF16)],
        lax.axis_index("seq").reshape(1),
        skip_gain,
        filters,
        forward,
        mix,
        twiddle,
        scalars=2,
    )

    message, gate = call(
        project_kernel,
        [shape((seq_count, 80, width), BF16), shape((rows, width), F32)],
        chan_index,
        *pieces,
        norm_gain.reshape(-1, width),
        in_weight,
        short_kernel,
        scalars=1,
        scratch=[
            pltpu.VMEM((rows + HALO, 3 * width), F32),
            pltpu.VMEM((8 * width, 3 * width), BF16),
            turned,
        ],
        cost=pl.CostEstimate(flops=int(PROJECT_FLOPS), bytes_accessed=1, transcendentals=0),
    )
    message, filters = after(message, filters)
    signal = lax.all_to_all(message, "seq", 0, 0)
    conv = call(
        conv_kernel, shape((seq_count, 80, width), BF16), signal, gain, forward, mix, twiddle, backward
    )
    columns = [around(column, steps) for column, steps in zip(columns, (1, 2, 3))]
    conv, *columns = after(conv, *columns)
    conv = lax.all_to_all(conv, "seq", 0, 0)
    gated, mine, theirs = call(
        gate_kernel,
        [shape((rows, width), BF16)] + [shape((4 * width, width), BF16)] * 2,
        chan_index,
        conv,
        gate,
        out_weight,
        *columns,
        scalars=1,
        scratch=[turned],
    )
    return call(output_kernel, shape((rows, width), F32), *gather(gated), mine, across(theirs), tokens)


def solution(mesh):
    return jax.shard_map(
        local,
        mesh=mesh,
        in_specs=(
            P("seq", "chan"),
            P(),
            P(None, None, "chan"),
            P(None, None, "chan"),
            P("seq", "chan"),
            P("seq", "chan"),
            P("chan"),
            P("chan", None),
        ),
        out_specs=P("seq", "chan"),
        check_vma=False,
    )
```

```python
import functools

import jax
import jax.numpy as jnp
import ml_dtypes
import numpy as np
from jax import lax
from jax.experimental import pallas as pl
from jax.experimental.pallas import tpu as pltpu
from jax.sharding import PartitionSpec as P

HALO = 16
PROJECT_FLOPS = 1.5e9
LANES = 128
VMEM_LIMIT = 16 * 1024 * 1024
VMEM = pl.BlockSpec(memory_space=pltpu.VMEM)
F32 = jnp.float32
BF16 = jnp.bfloat16


def split_np(table):
    high = table.astype(np.float32).astype(ml_dtypes.bfloat16)
    low = (table - high.astype(np.float64)).astype(np.float32).astype(ml_dtypes.bfloat16)
    return high, low


@functools.cache
def tables():
    n = LANES
    period = 2 * n * n
    k = np.arange(n, dtype=np.float64)
    first = 2 * np.pi * np.outer(k + 0.5, k) / (2 * n)
    forward = np.concatenate([np.cos(first), -np.sin(first)], axis=0)
    second = 2 * np.pi * np.outer(k, k) / n
    cosine, sine = np.cos(second), np.sin(second)
    mix = np.block([[cosine, -sine], [sine, cosine]])
    turn = 2 * np.pi * np.outer(k + 0.5, k) / period
    twiddle = np.stack([np.cos(turn), -np.sin(turn)]).astype(np.float32)
    forward_hi, forward_lo = split_np(forward)
    mix_hi, mix_lo = split_np(mix)
    return {
        "forward": np.concatenate([forward_hi, forward_lo], axis=1),
        "mix": np.concatenate([mix_hi, mix_lo], axis=0),
        "twiddle": twiddle,
    }


def halves(value):
    high = value.astype(BF16)
    return high, (value - high.astype(F32)).astype(BF16)


def dot(left, right):
    return jnp.dot(left, right, preferred_element_type=F32)


def left_dot(table_ref, value):
    high, low = halves(value)
    depth = value.shape[0]
    table_hi, table_lo = table_ref[:, :depth], table_ref[:, depth:]
    return dot(jnp.concatenate([table_hi, table_lo, table_hi], axis=1), jnp.concatenate([high, high, low], axis=0))


def right_dot(value, table_ref):
    high, low = halves(value)
    depth = value.shape[1]
    table_hi, table_lo = table_ref[:depth], table_ref[depth:]
    return dot(jnp.concatenate([high, low, high], axis=1), jnp.concatenate([table_hi, table_hi, table_lo], axis=0))


def transform(sequences, forward_ref, mix_ref, twiddle_ref):
    n = LANES
    value = jnp.concatenate(sequences, axis=1)
    parts = dot(forward_ref[...], jnp.concatenate([value, value], axis=0))
    cosine, sine = twiddle_ref[0], twiddle_ref[1]
    rows = []
    for i in range(len(sequences)):
        real = parts[:n, i * n : (i + 1) * n]
        imag = parts[n:, i * n : (i + 1) * n]
        rows.append(jnp.concatenate([real * cosine - imag * sine, real * sine + imag * cosine], axis=1))
    return right_dot(jnp.concatenate(rows, axis=0), mix_ref)


def fetch(pairs, sems):
    copies = [pltpu.make_async_copy(source, target, sems.at[i]) for i, (source, target) in enumerate(pairs)]
    for copy in copies:
        copy.start()
    return copies


def spread_kernel(index_ref, fwd_ref, bwd_ref, weight_ref, out_ref, *refs):
    columns_refs, (held_ref, turned_ref, sems, column_sems) = refs[:3], refs[3:]
    step = 2 * LANES
    places = [(which, start) for which in range(2) for start in range(0, fwd_ref.shape[0], step)]
    copies = fetch(
        [
            ((fwd_ref, bwd_ref)[which].at[pl.ds(start, step), :], held_ref.at[which, pl.ds(start, step), :])
            for which, start in places
        ],
        sems,
    )
    z = index_ref[0] // 2
    columns = fetch(
        [
            (weight_ref.at[:, pl.ds(pl.multiple_of((z + steps) % 4 * 2 * LANES, 2 * LANES), 2 * LANES)], columns_ref)
            for steps, columns_ref in zip((1, 2, 3), columns_refs)
        ],
        column_sems,
    )
    for copy, (which, start) in zip(copies, places):
        copy.wait()
        for block in range(start // LANES, (start + step) // LANES):
            turned = held_ref[which, block * LANES : (block + 1) * LANES, :].T
            turned_ref[which, pl.ds(block, LANES, stride=8), :] = turned
        if start + step == fwd_ref.shape[0]:
            out_ref[:, which * 64 : (which + 1) * 64, :] = turned_round(turned_ref[which].reshape(16, 64, LANES)).astype(BF16)
    for copy in columns:
        copy.wait()


def turned_round(value):
    return jnp.concatenate([value[15 - j : 16 - j] for j in range(16)], axis=0)


def exchange(value):
    return lax.all_to_all(value, "seq", 0, 0, axis_index_groups=[list(range(15, -1, -1))])


def channel_pair(ref, start):
    both = turned_round(ref[:, start : start + 16, :].astype(F32))
    return both[:, :8], both[:, 8:]


def filter_kernel(index_ref, skip_ref, filt_ref, forward_ref, mix_ref, twiddle_ref, gain_ref, backward_ref):
    n = LANES
    first_channel = index_ref[0] * 8
    for half in range(2):
        backward_ref[:, 2 * n * half : 2 * n * (half + 1)] = forward_ref[:, n * half : n * (half + 1)].astype(F32).T.astype(BF16)
    row = mix_ref[:8, :].astype(F32) + mix_ref[2 * n : 2 * n + 8, :].astype(F32)
    row_real, row_imag = row[1:2, :n], -row[1:2, n:]
    column_real, column_imag = twiddle_ref[0, :, 1:2], -twiddle_ref[1, :, 1:2]
    cosine = column_real * row_real - column_imag * row_imag
    sine = column_real * row_imag + column_imag * row_real
    for c in range(0, 8, 2):
        forth, back = [channel_pair(filt_ref, 64 * which + 8 * c) for which in range(2)]
        spectra = transform(
            [part.reshape(n, n).astype(BF16) for part in forth + back], forward_ref, mix_ref, twiddle_ref
        )
        for i in range(2):
            forth_rows = slice(i * n, (i + 1) * n)
            back_rows = slice((2 + i) * n, (3 + i) * n)
            back_real, back_imag = spectra[back_rows, :n], -spectra[back_rows, n:]
            gain_ref[c + i, 0] = spectra[forth_rows, :n] + (back_real * cosine - back_imag * sine) + skip_ref[first_channel + c + i]
            gain_ref[c + i, 1] = spectra[forth_rows, n:] + (back_real * sine + back_imag * cosine)


def conv_kernel(sig_ref, gain_ref, forward_ref, mix_ref, twiddle_ref, backward_ref, out_ref):
    n = LANES
    extra_high, extra_low = channel_pair(sig_ref, 64)
    extra = extra_high + extra_low
    before = jnp.concatenate([jnp.zeros((1, 8, n), F32), extra[:-1]], axis=0)
    high = before.astype(BF16).astype(F32)
    out_ref[:, 64:, :] = turned_round(jnp.concatenate([high, before - high], axis=1)).astype(BF16)
    before = before.reshape(n, n)
    mixes = extra.reshape(n, n) + pltpu.roll(before, n - 4, 1)
    first = (mixes * pltpu.roll(mixes, n - 2, 1)).reshape(16, 8, n)
    at_first = jnp.logical_and(
        lax.broadcasted_iota(jnp.int32, (16, 8, n), 1) == 0, lax.broadcasted_iota(jnp.int32, (16, 8, n), 2) < 2
    )
    cosine, sine = twiddle_ref[0], twiddle_ref[1]
    sequences = []
    for c in range(0, 8, 2):
        for i, part in enumerate(channel_pair(sig_ref, 8 * c)):
            sequences.append(jnp.where(at_first, first[:, c + i : c + i + 1, :], part).reshape(n, n).astype(BF16))
    spectra = transform(sequences, forward_ref, mix_ref, twiddle_ref)
    rows = []
    for c in range(8):
        real, imag = spectra[c * n : (c + 1) * n, :n], spectra[c * n : (c + 1) * n, n:]
        gain_real, gain_imag = gain_ref[c, 0], gain_ref[c, 1]
        rows.append(
            jnp.concatenate([real * gain_real - imag * gain_imag, -(real * gain_imag + imag * gain_real)], axis=1)
        )
    parts = right_dot(jnp.concatenate(rows, axis=0), mix_ref)
    columns = []
    for c in range(8):
        real, imag = parts[c * n : (c + 1) * n, :n], parts[c * n : (c + 1) * n, n:]
        columns.append(jnp.concatenate([real * cosine - imag * sine, -(real * sine + imag * cosine)], axis=0))
    times = left_dot(backward_ref, jnp.concatenate(columns, axis=1)) * (1.0 / (n * n))
    blocks = [times[:, c * n : (c + 1) * n].reshape(16, 8, n) for c in range(8)]
    out_ref[:, :64, :] = turned_round(jnp.concatenate(blocks, axis=1)).astype(BF16)


def piece_block(j, z, core):
    return (z + 4 - j % 4) % 4 * 2 + (core if j < 4 else 1 - core)


def project_kernel(index_ref, *refs):
    pieces, refs = refs[:8], refs[8:]
    gain_ref, weight_ref, short_ref, message_ref, gate_ref, projected_ref, stacked_ref, turned_ref = refs
    rows, width = pieces[0].shape
    z, core = index_ref[0] // 2, index_ref[0] % 2
    gains = []
    for j in range(8):
        block = piece_block(j, z, core)
        gains.append(gain_ref[pl.ds(block, 1), :])
        source = pl.ds(pl.multiple_of(block * width, width), width)
        for k in range(3):
            stacked_ref[j * width : (j + 1) * width, k * width : (k + 1) * width] = weight_ref[k, source, :]
    projected_ref[:HALO, :] = jnp.zeros((HALO, 3 * width), F32)
    step = 512
    for start in range(0, rows, step):
        parts = [piece[start : start + step, :].astype(F32) for piece in pieces]
        total = sum(part * part for part in parts)
        inv_rms = lax.rsqrt(jnp.sum(total, axis=1, keepdims=True) * (1.0 / (8 * width)) + 1e-05)
        normed = jnp.concatenate([(part * inv_rms * gain).astype(BF16) for part, gain in zip(parts, gains)], axis=1)
        projected_ref[HALO + start : HALO + start + step, :] = dot(normed, stacked_ref[...])
    taps = [[short_ref[i, j : j + 1, :] for j in range(3)] for i in range(3)]
    for block in range(rows // LANES):
        start = block * LANES
        mixes = []
        for j in range(3):
            columns = slice(j * width, (j + 1) * width)
            mixes.append(
                sum(
                    taps[i][j] * projected_ref[HALO + start - i : HALO + start - i + LANES, columns]
                    for i in range(3)
                )
            )
        turned_ref[pl.ds(block, LANES, stride=8), :] = (mixes[0] * mixes[1]).T
        gate_ref[start : start + LANES, :] = mixes[2]
        if block == 0:
            early = [mixes[0][:2], mixes[1][:2]]
    later = []
    for j in range(3):
        columns = slice(j * width, (j + 1) * width)
        last = projected_ref[HALO + rows - 1 : HALO + rows, columns]
        before = projected_ref[HALO + rows - 2 : HALO + rows - 1, columns]
        later.append(jnp.concatenate([taps[1][j] * last + taps[2][j] * before, taps[2][j] * last], axis=0))
    extra = jnp.concatenate(early + later + [jnp.zeros((LANES - 10, width), F32)], axis=0).T
    high = extra.astype(BF16).astype(F32)
    message_ref[:, :64, :] = turned_round(turned_ref[...].reshape(16, 64, LANES)).astype(BF16)
    message_ref[:, 64:, :] = turned_round(
        jnp.concatenate([high.reshape(16, 8, LANES), (extra - high).reshape(16, 8, LANES)], axis=1)
    ).astype(BF16)


def gate_kernel(index_ref, conv_ref, gate_ref, weight_ref, *refs):
    columns_refs, (out_ref, mine_ref, theirs_ref, turned_ref) = refs[:3], refs[3:]
    z, core = index_ref[0] // 2, index_ref[0] % 2
    for k in range(4):
        for ref, c in ((mine_ref, core), (theirs_ref, 1 - core)):
            start = c * LANES if k else (2 * z + c) * LANES
            source = columns_refs[k - 1] if k else weight_ref
            ref[k * LANES : (k + 1) * LANES, :] = source[:, pl.ds(pl.multiple_of(start, LANES), LANES)]
    turned_ref[...] = turned_round(conv_ref[:, :64, :].astype(F32)).reshape(turned_ref.shape)
    extra_high, extra_low = channel_pair(conv_ref, 64)
    late = (extra_high + extra_low).reshape(LANES, LANES).T[8:10]
    for block in range(gate_ref.shape[0] // LANES):
        rows = slice(block * LANES, (block + 1) * LANES)
        conv = turned_ref[pl.ds(block, LANES, stride=8), :].T
        gate = gate_ref[rows, :]
        if block == 0:
            gate = jnp.concatenate([gate[:2] + late, gate[2:]], axis=0)
        out_ref[rows, :] = (gate * conv).astype(BF16)


def output_kernel(*refs):
    gated, mine_ref, theirs_ref, tokens_ref, out_ref = refs[:8], *refs[8:]
    weight = jnp.concatenate([mine_ref[...], theirs_ref[...]], axis=0)
    step = 256
    for start in range(0, out_ref.shape[0], step):
        piece = slice(start, start + step)
        product = dot(jnp.concatenate([ref[piece, :] for ref in gated], axis=1), weight)
        out_ref[piece, :] = tokens_ref[piece, :].astype(F32) + product


def around(value, steps):
    count = lax.axis_size("chan")
    return lax.ppermute(value, "chan", [(i, (i + 2 * steps) % count) for i in range(count)])


def across(value):
    return lax.ppermute(value, "chan", [(i, i ^ 1) for i in range(lax.axis_size("chan"))])


def gather(value):
    mine = [value] + [around(value, steps) for steps in (1, 2, 3)]
    return mine + [across(piece) for piece in mine]


def after(*values):
    return lax.optimization_barrier(values)


def call(kernel, shapes, *operands, scalars=0, outside=(), scratch=(), cost=None):
    spaces = [pltpu.SMEM if i < scalars else pltpu.HBM if i in outside else pltpu.VMEM for i in range(len(operands))]
    operands = [
        pltpu.with_memory_space_constraint(operand, space) if space is pltpu.HBM else operand
        for operand, space in zip(operands, spaces)
    ]
    return pl.pallas_call(
        kernel,
        out_shape=shapes,
        in_specs=[pl.BlockSpec(memory_space=space) for space in spaces],
        out_specs=jax.tree.map(lambda _: VMEM, shapes),
        scratch_shapes=scratch,
        cost_estimate=cost,
        compiler_params=pltpu.CompilerParams(vmem_limit_bytes=VMEM_LIMIT),
    )(*operands)


def local(tokens, norm_gain, in_weight, short_kernel, filter_fwd, filter_bwd, skip_gain, out_weight):
    seq_count = lax.axis_size("seq")
    chan_index = lax.axis_index("chan").reshape(1)
    rows, width = tokens.shape
    shape = jax.ShapeDtypeStruct
    turned = pltpu.VMEM((rows, width), F32)

    spread, *columns = call(
        spread_kernel,
        [shape((seq_count, 128, width), BF16)] + [shape((width, 2 * width), BF16)] * 3,
        chan_index,
        filter_fwd,
        filter_bwd,
        out_weight,
        scalars=1,
        outside=(1, 2, 3),
        scratch=[pltpu.VMEM((2, rows, width), F32)] * 2
        + [pltpu.SemaphoreType.DMA((8,)), pltpu.SemaphoreType.DMA((3,))],
    )
    pieces = [tokens] + [around(tokens, steps) for steps in (1, 2, 3)]
    pieces = pieces + [across(piece) for piece in pieces]
    filters = exchange(spread)
    forward, mix, twiddle = [jnp.asarray(tables()[name]) for name in ("forward", "mix", "twiddle")]
    gain, backward = call(
        filter_kernel,
        [shape((8, 2, LANES, LANES), F32), shape((LANES, 4 * LANES), BF16)],
        lax.axis_index("seq").reshape(1),
        skip_gain,
        filters,
        forward,
        mix,
        twiddle,
        scalars=2,
    )

    message, gate = call(
        project_kernel,
        [shape((seq_count, 80, width), BF16), shape((rows, width), F32)],
        chan_index,
        *pieces,
        norm_gain.reshape(-1, width),
        in_weight,
        short_kernel,
        scalars=1,
        scratch=[
            pltpu.VMEM((rows + HALO, 3 * width), F32),
            pltpu.VMEM((8 * width, 3 * width), BF16),
            turned,
        ],
        cost=pl.CostEstimate(flops=int(PROJECT_FLOPS), bytes_accessed=1, transcendentals=0),
    )
    message, filters = after(message, filters)
    signal = exchange(message)
    conv = call(
        conv_kernel, shape((seq_count, 80, width), BF16), signal, gain, forward, mix, twiddle, backward
    )
    columns = [around(column, steps) for column, steps in zip(columns, (1, 2, 3))]
    conv, *columns = after(conv, *columns)
    conv = exchange(conv)
    gated, mine, theirs = call(
        gate_kernel,
        [shape((rows, width), BF16)] + [shape((4 * width, width), BF16)] * 2,
        chan_index,
        conv,
        gate,
        out_weight,
        *columns,
        scalars=1,
        scratch=[turned],
    )
    pieces = [gated] + [around(gated, steps) for steps in (1, 2, 3)]
    theirs, pieces[3] = after(across(theirs), pieces[3])
    pieces = pieces + [across(piece) for piece in pieces]
    return call(output_kernel, shape((rows, width), F32), *pieces, mine, theirs, tokens)


def solution(mesh):
    return jax.shard_map(
        local,
        mesh=mesh,
        in_specs=(
            P("seq", "chan"),
            P(),
            P(None, None, "chan"),
            P(None, None, "chan"),
            P("seq", "chan"),
            P("seq", "chan"),
            P("chan"),
            P("chan", None),
        ),
        out_specs=P("seq", "chan"),
        check_vma=False,
    )
```

```python
import functools

import jax
import jax.numpy as jnp
import ml_dtypes
import numpy as np
from jax import lax
from jax.experimental import pallas as pl
from jax.experimental.pallas import tpu as pltpu
from jax.sharding import PartitionSpec as P

HALO = 16
PROJECT_FLOPS = 1.5e9
LANES = 128
VMEM_LIMIT = 16 * 1024 * 1024
VMEM = pl.BlockSpec(memory_space=pltpu.VMEM)
F32 = jnp.float32
BF16 = jnp.bfloat16


def split_np(table):
    high = table.astype(np.float32).astype(ml_dtypes.bfloat16)
    low = (table - high.astype(np.float64)).astype(np.float32).astype(ml_dtypes.bfloat16)
    return high, low


@functools.cache
def tables():
    n = LANES
    period = 2 * n * n
    k = np.arange(n, dtype=np.float64)
    first = 2 * np.pi * np.outer(k + 0.5, k) / (2 * n)
    forward = np.concatenate([np.cos(first), -np.sin(first)], axis=0)
    second = 2 * np.pi * np.outer(k, k) / n
    cosine, sine = np.cos(second), np.sin(second)
    mix = np.block([[cosine, -sine], [sine, cosine]])
    turn = 2 * np.pi * np.outer(k + 0.5, k) / period
    twiddle = np.stack([np.cos(turn), -np.sin(turn)]).astype(np.float32)
    forward_hi, forward_lo = split_np(forward)
    mix_hi, mix_lo = split_np(mix)
    return {
        "forward": np.concatenate([forward_hi, forward_lo], axis=1),
        "mix": np.concatenate([mix_hi, mix_lo], axis=0),
        "twiddle": twiddle,
    }


def halves(value):
    high = value.astype(BF16)
    return high, (value - high.astype(F32)).astype(BF16)


def dot(left, right):
    return jnp.dot(left, right, preferred_element_type=F32)


def left_dot(table_ref, value):
    high, low = halves(value)
    depth = value.shape[0]
    table_hi, table_lo = table_ref[:, :depth], table_ref[:, depth:]
    return dot(jnp.concatenate([table_hi, table_lo, table_hi], axis=1), jnp.concatenate([high, high, low], axis=0))


def right_dot(value, table_ref):
    high, low = halves(value)
    depth = value.shape[1]
    table_hi, table_lo = table_ref[:depth], table_ref[depth:]
    return dot(jnp.concatenate([high, low, high], axis=1), jnp.concatenate([table_hi, table_hi, table_lo], axis=0))


def transform(sequences, forward_ref, mix_ref, twiddle_ref):
    n = LANES
    value = jnp.concatenate(sequences, axis=1)
    parts = dot(forward_ref[...], jnp.concatenate([value, value], axis=0))
    cosine, sine = twiddle_ref[0], twiddle_ref[1]
    rows = []
    for i in range(len(sequences)):
        real = parts[:n, i * n : (i + 1) * n]
        imag = parts[n:, i * n : (i + 1) * n]
        rows.append(jnp.concatenate([real * cosine - imag * sine, real * sine + imag * cosine], axis=1))
    return right_dot(jnp.concatenate(rows, axis=0), mix_ref)


def fetch(pairs, sems):
    copies = [pltpu.make_async_copy(source, target, sems.at[i]) for i, (source, target) in enumerate(pairs)]
    for copy in copies:
        copy.start()
    return copies


def spread_kernel(index_ref, fwd_ref, bwd_ref, weight_ref, out_ref, *refs):
    columns_refs, (held_ref, turned_ref, sems, column_sems) = refs[:3], refs[3:]
    step = 2 * LANES
    places = [(which, start) for which in range(2) for start in range(0, fwd_ref.shape[0], step)]
    copies = fetch(
        [
            ((fwd_ref, bwd_ref)[which].at[pl.ds(start, step), :], held_ref.at[which, pl.ds(start, step), :])
            for which, start in places
        ],
        sems,
    )
    z = index_ref[0] // 2
    columns = fetch(
        [
            (weight_ref.at[:, pl.ds(pl.multiple_of((z + steps) % 4 * 2 * LANES, 2 * LANES), 2 * LANES)], columns_ref)
            for steps, columns_ref in zip((1, 2, 3), columns_refs)
        ],
        column_sems,
    )
    for copy, (which, start) in zip(copies, places):
        copy.wait()
        for block in range(start // LANES, (start + step) // LANES):
            turned = held_ref[which, block * LANES : (block + 1) * LANES, :].T
            turned_ref[which, pl.ds(block, LANES, stride=8), :] = turned
        if start + step == fwd_ref.shape[0]:
            out_ref[:, which * 64 : (which + 1) * 64, :] = turned_round(turned_ref[which].reshape(16, 64, LANES)).astype(BF16)
    for copy in columns:
        copy.wait()


def turned_round(value):
    return jnp.concatenate([value[15 - j : 16 - j] for j in range(16)], axis=0)


def exchange(value):
    return lax.all_to_all(value, "seq", 0, 0, axis_index_groups=[list(range(15, -1, -1))])


def channel_pair(ref, start):
    both = turned_round(ref[:, start : start + 16, :].astype(F32))
    return both[:, :8], both[:, 8:]


def filter_kernel(index_ref, skip_ref, filt_ref, forward_ref, mix_ref, twiddle_ref, gain_ref, backward_ref):
    n = LANES
    first_channel = index_ref[0] * 8
    for half in range(2):
        backward_ref[:, 2 * n * half : 2 * n * (half + 1)] = forward_ref[:, n * half : n * (half + 1)].astype(F32).T.astype(BF16)
    row = mix_ref[:8, :].astype(F32) + mix_ref[2 * n : 2 * n + 8, :].astype(F32)
    row_real, row_imag = row[1:2, :n], -row[1:2, n:]
    column_real, column_imag = twiddle_ref[0, :, 1:2], -twiddle_ref[1, :, 1:2]
    cosine = column_real * row_real - column_imag * row_imag
    sine = column_real * row_imag + column_imag * row_real
    for c in range(0, 8, 2):
        forth, back = [channel_pair(filt_ref, 64 * which + 8 * c) for which in range(2)]
        spectra = transform(
            [part.reshape(n, n).astype(BF16) for part in forth + back], forward_ref, mix_ref, twiddle_ref
        )
        for i in range(2):
            forth_rows = slice(i * n, (i + 1) * n)
            back_rows = slice((2 + i) * n, (3 + i) * n)
            back_real, back_imag = spectra[back_rows, :n], -spectra[back_rows, n:]
            gain_ref[c + i, 0] = spectra[forth_rows, :n] + (back_real * cosine - back_imag * sine) + skip_ref[first_channel + c + i]
            gain_ref[c + i, 1] = spectra[forth_rows, n:] + (back_real * sine + back_imag * cosine)


def conv_kernel(sig_ref, gain_ref, forward_ref, mix_ref, twiddle_ref, backward_ref, out_ref):
    n = LANES
    extra_high, extra_low = channel_pair(sig_ref, 64)
    extra = extra_high + extra_low
    before = jnp.concatenate([jnp.zeros((1, 8, n), F32), extra[:-1]], axis=0)
    high = before.astype(BF16).astype(F32)
    out_ref[:, 64:, :] = turned_round(jnp.concatenate([high, before - high], axis=1)).astype(BF16)
    before = before.reshape(n, n)
    mixes = extra.reshape(n, n) + pltpu.roll(before, n - 4, 1)
    first = (mixes * pltpu.roll(mixes, n - 2, 1)).reshape(16, 8, n)
    at_first = jnp.logical_and(
        lax.broadcasted_iota(jnp.int32, (16, 8, n), 1) == 0, lax.broadcasted_iota(jnp.int32, (16, 8, n), 2) < 2
    )
    cosine, sine = twiddle_ref[0], twiddle_ref[1]
    sequences = []
    for c in range(0, 8, 2):
        for i, part in enumerate(channel_pair(sig_ref, 8 * c)):
            sequences.append(jnp.where(at_first, first[:, c + i : c + i + 1, :], part).reshape(n, n).astype(BF16))
    spectra = transform(sequences, forward_ref, mix_ref, twiddle_ref)
    rows = []
    for c in range(8):
        real, imag = spectra[c * n : (c + 1) * n, :n], spectra[c * n : (c + 1) * n, n:]
        gain_real, gain_imag = gain_ref[c, 0], gain_ref[c, 1]
        rows.append(
            jnp.concatenate([real * gain_real - imag * gain_imag, -(real * gain_imag + imag * gain_real)], axis=1)
        )
    parts = right_dot(jnp.concatenate(rows, axis=0), mix_ref)
    columns = []
    for c in range(8):
        real, imag = parts[c * n : (c + 1) * n, :n], parts[c * n : (c + 1) * n, n:]
        columns.append(jnp.concatenate([real * cosine - imag * sine, -(real * sine + imag * cosine)], axis=0))
    times = left_dot(backward_ref, jnp.concatenate(columns, axis=1)) * (1.0 / (n * n))
    blocks = [times[:, c * n : (c + 1) * n].reshape(16, 8, n) for c in range(8)]
    out_ref[:, :64, :] = turned_round(jnp.concatenate(blocks, axis=1)).astype(BF16)


def piece_block(j, z, core):
    return (z + 4 - j % 4) % 4 * 2 + (core if j < 4 else 1 - core)


def project_kernel(index_ref, *refs):
    pieces, refs = refs[:8], refs[8:]
    gain_ref, weight_ref, short_ref, message_ref, gate_ref, projected_ref, stacked_ref, turned_ref = refs
    rows, width = pieces[0].shape
    z, core = index_ref[0] // 2, index_ref[0] % 2
    gains = []
    for j in range(8):
        block = piece_block(j, z, core)
        gains.append(gain_ref[pl.ds(block, 1), :])
        source = pl.ds(pl.multiple_of(block * width, width), width)
        for k in range(3):
            stacked_ref[j * width : (j + 1) * width, k * width : (k + 1) * width] = weight_ref[k, source, :]
    projected_ref[:HALO, :] = jnp.zeros((HALO, 3 * width), F32)
    step = 512
    for start in range(0, rows, step):
        parts = [piece[start : start + step, :].astype(F32) for piece in pieces]
        total = sum(part * part for part in parts)
        inv_rms = lax.rsqrt(jnp.sum(total, axis=1, keepdims=True) * (1.0 / (8 * width)) + 1e-05)
        normed = jnp.concatenate([(part * inv_rms * gain).astype(BF16) for part, gain in zip(parts, gains)], axis=1)
        projected_ref[HALO + start : HALO + start + step, :] = dot(normed, stacked_ref[...])
    taps = [[short_ref[i, j : j + 1, :] for j in range(3)] for i in range(3)]
    for block in range(rows // LANES):
        start = block * LANES
        mixes = []
        for j in range(3):
            columns = slice(j * width, (j + 1) * width)
            mixes.append(
                sum(
                    taps[i][j] * projected_ref[HALO + start - i : HALO + start - i + LANES, columns]
                    for i in range(3)
                )
            )
        turned_ref[pl.ds(block, LANES, stride=8), :] = (mixes[0] * mixes[1]).T
        gate_ref[start : start + LANES, :] = mixes[2]
        if block == 0:
            early = [mixes[0][:2], mixes[1][:2]]
    later = []
    for j in range(3):
        columns = slice(j * width, (j + 1) * width)
        last = projected_ref[HALO + rows - 1 : HALO + rows, columns]
        before = projected_ref[HALO + rows - 2 : HALO + rows - 1, columns]
        later.append(jnp.concatenate([taps[1][j] * last + taps[2][j] * before, taps[2][j] * last], axis=0))
    extra = jnp.concatenate(early + later + [jnp.zeros((LANES - 10, width), F32)], axis=0).T
    high = extra.astype(BF16).astype(F32)
    message_ref[:, :64, :] = turned_round(turned_ref[...].reshape(16, 64, LANES)).astype(BF16)
    message_ref[:, 64:, :] = turned_round(
        jnp.concatenate([high.reshape(16, 8, LANES), (extra - high).reshape(16, 8, LANES)], axis=1)
    ).astype(BF16)


def gate_kernel(index_ref, conv_ref, gate_ref, weight_ref, *refs):
    columns_refs, (out_ref, mine_ref, theirs_ref, turned_ref) = refs[:3], refs[3:]
    z, core = index_ref[0] // 2, index_ref[0] % 2
    for k in range(4):
        for ref, c in ((mine_ref, core), (theirs_ref, 1 - core)):
            start = c * LANES if k else (2 * z + c) * LANES
            source = columns_refs[k - 1] if k else weight_ref
            ref[k * LANES : (k + 1) * LANES, :] = source[:, pl.ds(pl.multiple_of(start, LANES), LANES)]
    turned_ref[...] = turned_round(conv_ref[:, :64, :].astype(F32)).reshape(turned_ref.shape)
    extra_high, extra_low = channel_pair(conv_ref, 64)
    late = (extra_high + extra_low).reshape(LANES, LANES).T[8:10]
    for block in range(gate_ref.shape[0] // LANES):
        rows = slice(block * LANES, (block + 1) * LANES)
        conv = turned_ref[pl.ds(block, LANES, stride=8), :].T
        gate = gate_ref[rows, :]
        if block == 0:
            gate = jnp.concatenate([gate[:2] + late, gate[2:]], axis=0)
        out_ref[rows, :] = (gate * conv).astype(BF16)


def output_kernel(*refs):
    gated, (mine_ref, theirs_ref, tokens_ref, out_ref, total_ref, sems) = refs[:8], refs[8:]
    weight = jnp.concatenate([mine_ref[...], theirs_ref[...]], axis=0)
    step = 256
    copies = []
    for start in range(0, total_ref.shape[0], step):
        piece = slice(start, start + step)
        product = dot(jnp.concatenate([ref[piece, :] for ref in gated], axis=1), weight)
        total_ref[piece, :] = tokens_ref[piece, :].astype(F32) + product
        part = pl.ds(start, step)
        copies.append(pltpu.make_async_copy(total_ref.at[part, :], out_ref.at[part, :], sems.at[start // step]))
        copies[-1].start()
    for copy in copies:
        copy.wait()


def around(value, steps):
    count = lax.axis_size("chan")
    return lax.ppermute(value, "chan", [(i, (i + 2 * steps) % count) for i in range(count)])


def across(value):
    return lax.ppermute(value, "chan", [(i, i ^ 1) for i in range(lax.axis_size("chan"))])


def gather(value):
    mine = [value] + [around(value, steps) for steps in (1, 2, 3)]
    return mine + [across(piece) for piece in mine]


def after(*values):
    return lax.optimization_barrier(values)


def call(kernel, shapes, *operands, scalars=0, outside=(), written=(), scratch=(), cost=None):
    spaces = [pltpu.SMEM if i < scalars else pltpu.HBM if i in outside else pltpu.VMEM for i in range(len(operands))]
    operands = [
        pltpu.with_memory_space_constraint(operand, space) if space is pltpu.HBM else operand
        for operand, space in zip(operands, spaces)
    ]
    return pl.pallas_call(
        kernel,
        out_shape=list(shapes),
        in_specs=[pl.BlockSpec(memory_space=space) for space in spaces],
        out_specs=[pl.BlockSpec(memory_space=pl.ANY) if i in written else VMEM for i in range(len(shapes))],
        scratch_shapes=scratch,
        cost_estimate=cost,
        compiler_params=pltpu.CompilerParams(vmem_limit_bytes=VMEM_LIMIT),
    )(*operands)


def local(tokens, norm_gain, in_weight, short_kernel, filter_fwd, filter_bwd, skip_gain, out_weight):
    seq_count = lax.axis_size("seq")
    chan_index = lax.axis_index("chan").reshape(1)
    rows, width = tokens.shape
    shape = jax.ShapeDtypeStruct
    turned = pltpu.VMEM((rows, width), F32)

    spread, *columns = call(
        spread_kernel,
        [shape((seq_count, 128, width), BF16)] + [shape((width, 2 * width), BF16)] * 3,
        chan_index,
        filter_fwd,
        filter_bwd,
        out_weight,
        scalars=1,
        outside=(1, 2, 3),
        scratch=[pltpu.VMEM((2, rows, width), F32)] * 2
        + [pltpu.SemaphoreType.DMA((8,)), pltpu.SemaphoreType.DMA((3,))],
    )
    pieces = [tokens] + [around(tokens, steps) for steps in (1, 2, 3)]
    pieces = pieces + [across(piece) for piece in pieces]
    filters = exchange(spread)
    forward, mix, twiddle = [jnp.asarray(tables()[name]) for name in ("forward", "mix", "twiddle")]
    gain, backward = call(
        filter_kernel,
        [shape((8, 2, LANES, LANES), F32), shape((LANES, 4 * LANES), BF16)],
        lax.axis_index("seq").reshape(1),
        skip_gain,
        filters,
        forward,
        mix,
        twiddle,
        scalars=2,
    )

    message, gate = call(
        project_kernel,
        [shape((seq_count, 80, width), BF16), shape((rows, width), F32)],
        chan_index,
        *pieces,
        norm_gain.reshape(-1, width),
        in_weight,
        short_kernel,
        scalars=1,
        scratch=[
            pltpu.VMEM((rows + HALO, 3 * width), F32),
            pltpu.VMEM((8 * width, 3 * width), BF16),
            turned,
        ],
        cost=pl.CostEstimate(flops=int(PROJECT_FLOPS), bytes_accessed=1, transcendentals=0),
    )
    message, filters = after(message, filters)
    signal = exchange(message)
    (conv,) = call(
        conv_kernel, [shape((seq_count, 80, width), BF16)], signal, gain, forward, mix, twiddle, backward
    )
    columns = [around(column, steps) for column, steps in zip(columns, (1, 2, 3))]
    conv, *columns = after(conv, *columns)
    conv = exchange(conv)
    gated, mine, theirs = call(
        gate_kernel,
        [shape((rows, width), BF16)] + [shape((4 * width, width), BF16)] * 2,
        chan_index,
        conv,
        gate,
        out_weight,
        *columns,
        scalars=1,
        scratch=[turned],
    )
    pieces = [gated] + [around(gated, steps) for steps in (1, 2, 3)]
    theirs, pieces[3] = after(across(theirs), pieces[3])
    pieces = pieces + [across(piece) for piece in pieces]
    (result,) = call(
        output_kernel,
        [shape((rows, width), F32)],
        *pieces,
        mine,
        theirs,
        tokens,
        written=(0,),
        scratch=[turned, pltpu.SemaphoreType.DMA((rows // 256,))],
    )
    return result


def solution(mesh):
    return jax.shard_map(
        local,
        mesh=mesh,
        in_specs=(
            P("seq", "chan"),
            P(),
            P(None, None, "chan"),
            P(None, None, "chan"),
            P("seq", "chan"),
            P("seq", "chan"),
            P("chan"),
            P("chan", None),
        ),
        out_specs=P("seq", "chan"),
        check_vma=False,
    )
```

```python
import functools

import jax
import jax.numpy as jnp
import ml_dtypes
import numpy as np
from jax import lax
from jax.experimental import pallas as pl
from jax.experimental.pallas import tpu as pltpu
from jax.sharding import PartitionSpec as P

HALO = 16
PROJECT_FLOPS = 1.5e9
LANES = 128
VMEM_LIMIT = 16 * 1024 * 1024
VMEM = pl.BlockSpec(memory_space=pltpu.VMEM)
F32 = jnp.float32
BF16 = jnp.bfloat16


def split_np(table):
    high = table.astype(np.float32).astype(ml_dtypes.bfloat16)
    low = (table - high.astype(np.float64)).astype(np.float32).astype(ml_dtypes.bfloat16)
    return high, low


@functools.cache
def tables():
    n = LANES
    period = 2 * n * n
    k = np.arange(n, dtype=np.float64)
    first = 2 * np.pi * np.outer(k + 0.5, k) / (2 * n)
    forward = np.concatenate([np.cos(first), -np.sin(first)], axis=0)
    second = 2 * np.pi * np.outer(k, k) / n
    cosine, sine = np.cos(second), np.sin(second)
    mix = np.block([[cosine, -sine], [sine, cosine]])
    turn = 2 * np.pi * np.outer(k + 0.5, k) / period
    twiddle = np.stack([np.cos(turn), -np.sin(turn)]).astype(np.float32)
    forward_hi, forward_lo = split_np(forward)
    mix_hi, mix_lo = split_np(mix)
    return {
        "forward": np.concatenate([forward_hi, forward_lo], axis=1),
        "mix": np.concatenate([mix_hi, mix_lo], axis=0),
        "twiddle": twiddle,
    }


def halves(value):
    high = value.astype(BF16)
    return high, (value - high.astype(F32)).astype(BF16)


def dot(left, right):
    return jnp.dot(left, right, preferred_element_type=F32)


def left_dot(table_ref, value):
    high, low = halves(value)
    depth = value.shape[0]
    table_hi, table_lo = table_ref[:, :depth], table_ref[:, depth:]
    return dot(jnp.concatenate([table_hi, table_lo, table_hi], axis=1), jnp.concatenate([high, high, low], axis=0))


def right_dot(value, table_ref):
    high, low = halves(value)
    depth = value.shape[1]
    table_hi, table_lo = table_ref[:depth], table_ref[depth:]
    return dot(jnp.concatenate([high, low, high], axis=1), jnp.concatenate([table_hi, table_hi, table_lo], axis=0))


def transform(sequences, forward_ref, mix_ref, twiddle_ref):
    n = LANES
    value = jnp.concatenate(sequences, axis=1)
    parts = dot(forward_ref[...], jnp.concatenate([value, value], axis=0))
    cosine, sine = twiddle_ref[0], twiddle_ref[1]
    rows = []
    for i in range(len(sequences)):
        real = parts[:n, i * n : (i + 1) * n]
        imag = parts[n:, i * n : (i + 1) * n]
        rows.append(jnp.concatenate([real * cosine - imag * sine, real * sine + imag * cosine], axis=1))
    return right_dot(jnp.concatenate(rows, axis=0), mix_ref)


def fetch(pairs, sems):
    copies = [pltpu.make_async_copy(source, target, sems.at[i]) for i, (source, target) in enumerate(pairs)]
    for copy in copies:
        copy.start()
    return copies


def spread_kernel(index_ref, fwd_ref, bwd_ref, weight_ref, out_ref, *refs):
    columns_refs, (held_ref, turned_ref, sems, column_sems) = refs[:3], refs[3:]
    step = 2 * LANES
    places = [(which, start) for which in range(2) for start in range(0, fwd_ref.shape[0], step)]
    copies = fetch(
        [
            ((fwd_ref, bwd_ref)[which].at[pl.ds(start, step), :], held_ref.at[which, pl.ds(start, step), :])
            for which, start in places
        ],
        sems,
    )
    z = index_ref[0] // 2
    columns = fetch(
        [
            (weight_ref.at[:, pl.ds(pl.multiple_of((z + steps) % 4 * 2 * LANES, 2 * LANES), 2 * LANES)], columns_ref)
            for steps, columns_ref in zip((1, 2, 3), columns_refs)
        ],
        column_sems,
    )
    for copy, (which, start) in zip(copies, places):
        copy.wait()
        for block in range(start // LANES, (start + step) // LANES):
            turned = held_ref[which, block * LANES : (block + 1) * LANES, :].T
            turned_ref[which, pl.ds(block, LANES, stride=8), :] = turned
        if start + step == fwd_ref.shape[0]:
            out_ref[:, which * 64 : (which + 1) * 64, :] = turned_round(turned_ref[which].reshape(16, 64, LANES)).astype(BF16)
    for copy in columns:
        copy.wait()


def turned_round(value):
    return jnp.concatenate([value[15 - j : 16 - j] for j in range(16)], axis=0)


def exchange(value):
    return lax.all_to_all(value, "seq", 0, 0, axis_index_groups=[list(range(15, -1, -1))])


def channel_pair(ref, start):
    both = turned_round(ref[:, start : start + 16, :].astype(F32))
    return both[:, :8], both[:, 8:]


def filter_kernel(index_ref, skip_ref, filt_ref, forward_ref, mix_ref, twiddle_ref, gain_ref, backward_ref):
    n = LANES
    first_channel = index_ref[0] * 8
    for half in range(2):
        backward_ref[:, 2 * n * half : 2 * n * (half + 1)] = forward_ref[:, n * half : n * (half + 1)].astype(F32).T.astype(BF16)
    row = mix_ref[:8, :].astype(F32) + mix_ref[2 * n : 2 * n + 8, :].astype(F32)
    row_real, row_imag = row[1:2, :n], -row[1:2, n:]
    column_real, column_imag = twiddle_ref[0, :, 1:2], -twiddle_ref[1, :, 1:2]
    cosine = column_real * row_real - column_imag * row_imag
    sine = column_real * row_imag + column_imag * row_real
    for c in range(0, 8, 2):
        forth, back = [channel_pair(filt_ref, 64 * which + 8 * c) for which in range(2)]
        spectra = transform(
            [part.reshape(n, n).astype(BF16) for part in forth + back], forward_ref, mix_ref, twiddle_ref
        )
        for i in range(2):
            forth_rows = slice(i * n, (i + 1) * n)
            back_rows = slice((2 + i) * n, (3 + i) * n)
            back_real, back_imag = spectra[back_rows, :n], -spectra[back_rows, n:]
            gain_ref[c + i, 0] = spectra[forth_rows, :n] + (back_real * cosine - back_imag * sine) + skip_ref[first_channel + c + i]
            gain_ref[c + i, 1] = spectra[forth_rows, n:] + (back_real * sine + back_imag * cosine)


def conv_kernel(sig_ref, gain_ref, forward_ref, mix_ref, twiddle_ref, backward_ref, out_ref):
    n = LANES
    extra_high, extra_low = channel_pair(sig_ref, 64)
    extra = extra_high + extra_low
    before = jnp.concatenate([jnp.zeros((1, 8, n), F32), extra[:-1]], axis=0)
    high = before.astype(BF16).astype(F32)
    out_ref[:, 64:, :] = turned_round(jnp.concatenate([high, before - high], axis=1)).astype(BF16)
    before = before.reshape(n, n)
    mixes = extra.reshape(n, n) + pltpu.roll(before, n - 4, 1)
    first = (mixes * pltpu.roll(mixes, n - 2, 1)).reshape(16, 8, n)
    at_first = jnp.logical_and(
        lax.broadcasted_iota(jnp.int32, (16, 8, n), 1) == 0, lax.broadcasted_iota(jnp.int32, (16, 8, n), 2) < 2
    )
    cosine, sine = twiddle_ref[0], twiddle_ref[1]
    sequences = []
    for c in range(0, 8, 2):
        for i, part in enumerate(channel_pair(sig_ref, 8 * c)):
            sequences.append(jnp.where(at_first, first[:, c + i : c + i + 1, :], part).reshape(n, n).astype(BF16))
    spectra = transform(sequences, forward_ref, mix_ref, twiddle_ref)
    rows = []
    for c in range(8):
        real, imag = spectra[c * n : (c + 1) * n, :n], spectra[c * n : (c + 1) * n, n:]
        gain_real, gain_imag = gain_ref[c, 0], gain_ref[c, 1]
        rows.append(
            jnp.concatenate([real * gain_real - imag * gain_imag, -(real * gain_imag + imag * gain_real)], axis=1)
        )
    parts = right_dot(jnp.concatenate(rows, axis=0), mix_ref)
    columns = []
    for c in range(8):
        real, imag = parts[c * n : (c + 1) * n, :n], parts[c * n : (c + 1) * n, n:]
        columns.append(jnp.concatenate([real * cosine - imag * sine, -(real * sine + imag * cosine)], axis=0))
    times = left_dot(backward_ref, jnp.concatenate(columns, axis=1)) * (1.0 / (n * n))
    blocks = [times[:, c * n : (c + 1) * n].reshape(16, 8, n) for c in range(8)]
    out_ref[:, :64, :] = turned_round(jnp.concatenate(blocks, axis=1)).astype(BF16)


def piece_block(j, z, core):
    return (z + 4 - j % 4) % 4 * 2 + (core if j < 4 else 1 - core)


def project_kernel(index_ref, *refs):
    pieces, refs = refs[:8], refs[8:]
    gain_ref, weight_ref, short_ref, message_ref, gate_ref, projected_ref, stacked_ref, turned_ref = refs
    rows, width = pieces[0].shape
    z, core = index_ref[0] // 2, index_ref[0] % 2
    gains = []
    for j in range(8):
        block = piece_block(j, z, core)
        gains.append(gain_ref[pl.ds(block, 1), :])
        source = pl.ds(pl.multiple_of(block * width, width), width)
        for k in range(3):
            stacked_ref[j * width : (j + 1) * width, k * width : (k + 1) * width] = weight_ref[k, source, :]
    projected_ref[:HALO, :] = jnp.zeros((HALO, 3 * width), F32)
    step = 512
    for start in range(0, rows, step):
        parts = [piece[start : start + step, :].astype(F32) for piece in pieces]
        total = sum(part * part for part in parts)
        inv_rms = lax.rsqrt(jnp.sum(total, axis=1, keepdims=True) * (1.0 / (8 * width)) + 1e-05)
        normed = jnp.concatenate([(part * inv_rms * gain).astype(BF16) for part, gain in zip(parts, gains)], axis=1)
        projected_ref[HALO + start : HALO + start + step, :] = dot(normed, stacked_ref[...])
    taps = [[short_ref[i, j : j + 1, :] for j in range(3)] for i in range(3)]
    for block in range(rows // LANES):
        start = block * LANES
        mixes = []
        for j in range(3):
            columns = slice(j * width, (j + 1) * width)
            mixes.append(
                sum(
                    taps[i][j] * projected_ref[HALO + start - i : HALO + start - i + LANES, columns]
                    for i in range(3)
                )
            )
        turned_ref[pl.ds(block, LANES, stride=8), :] = (mixes[0] * mixes[1]).T
        gate_ref[start : start + LANES, :] = mixes[2]
        if block == 0:
            early = [mixes[0][:2], mixes[1][:2]]
    later = []
    for j in range(3):
        columns = slice(j * width, (j + 1) * width)
        last = projected_ref[HALO + rows - 1 : HALO + rows, columns]
        before = projected_ref[HALO + rows - 2 : HALO + rows - 1, columns]
        later.append(jnp.concatenate([taps[1][j] * last + taps[2][j] * before, taps[2][j] * last], axis=0))
    extra = jnp.concatenate(early + later + [jnp.zeros((LANES - 10, width), F32)], axis=0).T
    high = extra.astype(BF16).astype(F32)
    message_ref[:, :64, :] = turned_round(turned_ref[...].reshape(16, 64, LANES)).astype(BF16)
    message_ref[:, 64:, :] = turned_round(
        jnp.concatenate([high.reshape(16, 8, LANES), (extra - high).reshape(16, 8, LANES)], axis=1)
    ).astype(BF16)


def gate_kernel(index_ref, conv_ref, gate_ref, weight_ref, *refs):
    columns_refs, (out_ref, mine_ref, theirs_ref, turned_ref) = refs[:3], refs[3:]
    z, core = index_ref[0] // 2, index_ref[0] % 2
    for k in range(4):
        for ref, c in ((mine_ref, core), (theirs_ref, 1 - core)):
            start = c * LANES if k else (2 * z + c) * LANES
            source = columns_refs[k - 1] if k else weight_ref
            ref[k * LANES : (k + 1) * LANES, :] = source[:, pl.ds(pl.multiple_of(start, LANES), LANES)]
    turned_ref[...] = turned_round(conv_ref[:, :64, :].astype(F32)).reshape(turned_ref.shape)
    extra_high, extra_low = channel_pair(conv_ref, 64)
    late = (extra_high + extra_low).reshape(LANES, LANES).T[8:10]
    for block in range(gate_ref.shape[0] // LANES):
        rows = slice(block * LANES, (block + 1) * LANES)
        conv = turned_ref[pl.ds(block, LANES, stride=8), :].T
        gate = gate_ref[rows, :]
        if block == 0:
            gate = jnp.concatenate([gate[:2] + late, gate[2:]], axis=0)
        out_ref[rows, :] = (gate * conv).astype(BF16)


def output_kernel(*refs):
    gated, (mine_ref, theirs_ref, tokens_ref, out_ref, total_ref, sems) = refs[:8], refs[8:]
    weight = jnp.concatenate([mine_ref[...], theirs_ref[...]], axis=0)
    step = 256
    copies = []
    for start in range(0, total_ref.shape[0], step):
        piece = slice(start, start + step)
        product = dot(jnp.concatenate([ref[piece, :] for ref in gated], axis=1), weight)
        total_ref[piece, :] = tokens_ref[piece, :].astype(F32) + product
        part = pl.ds(start, step)
        copies.append(pltpu.make_async_copy(total_ref.at[part, :], out_ref.at[part, :], sems.at[start // step]))
        copies[-1].start()
    for copy in copies:
        copy.wait()


def around(value, steps):
    count = lax.axis_size("chan")
    return lax.ppermute(value, "chan", [(i, (i + 2 * steps) % count) for i in range(count)])


def across(value):
    return lax.ppermute(value, "chan", [(i, i ^ 1) for i in range(lax.axis_size("chan"))])


def gather(value):
    mine = [value] + [around(value, steps) for steps in (1, 2, 3)]
    return mine + [across(piece) for piece in mine]


def after(*values):
    return lax.optimization_barrier(values)


def call(kernel, shapes, *operands, scalars=0, outside=(), written=(), scratch=(), cost=None):
    spaces = [pltpu.SMEM if i < scalars else pltpu.HBM if i in outside else pltpu.VMEM for i in range(len(operands))]
    operands = [
        pltpu.with_memory_space_constraint(operand, space) if space is pltpu.HBM else operand
        for operand, space in zip(operands, spaces)
    ]
    return pl.pallas_call(
        kernel,
        out_shape=list(shapes),
        in_specs=[pl.BlockSpec(memory_space=space) for space in spaces],
        out_specs=[pl.BlockSpec(memory_space=pl.ANY) if i in written else VMEM for i in range(len(shapes))],
        scratch_shapes=scratch,
        cost_estimate=cost,
        compiler_params=pltpu.CompilerParams(vmem_limit_bytes=VMEM_LIMIT),
    )(*operands)


def local(tokens, norm_gain, in_weight, short_kernel, filter_fwd, filter_bwd, skip_gain, out_weight):
    seq_count = lax.axis_size("seq")
    chan_index = lax.axis_index("chan").reshape(1)
    rows, width = tokens.shape
    shape = jax.ShapeDtypeStruct
    turned = pltpu.VMEM((rows, width), F32)

    spread, *columns = call(
        spread_kernel,
        [shape((seq_count, 128, width), BF16)] + [shape((width, 2 * width), BF16)] * 3,
        chan_index,
        filter_fwd,
        filter_bwd,
        out_weight,
        scalars=1,
        outside=(1, 2, 3),
        scratch=[pltpu.VMEM((2, rows, width), F32)] * 2
        + [pltpu.SemaphoreType.DMA((8,)), pltpu.SemaphoreType.DMA((3,))],
    )
    pieces = [tokens] + [around(tokens, steps) for steps in (1, 2, 3)]
    pieces = pieces + [across(piece) for piece in pieces]
    filters = exchange(spread)
    forward, mix, twiddle = [jnp.asarray(tables()[name]) for name in ("forward", "mix", "twiddle")]
    gain, backward = call(
        filter_kernel,
        [shape((8, 2, LANES, LANES), F32), shape((LANES, 4 * LANES), BF16)],
        lax.axis_index("seq").reshape(1),
        skip_gain,
        filters,
        forward,
        mix,
        twiddle,
        scalars=2,
    )

    message, gate = call(
        project_kernel,
        [shape((seq_count, 80, width), BF16), shape((rows, width), F32)],
        chan_index,
        *pieces,
        norm_gain.reshape(-1, width),
        in_weight,
        short_kernel,
        scalars=1,
        scratch=[
            pltpu.VMEM((rows + HALO, 3 * width), F32),
            pltpu.VMEM((8 * width, 3 * width), BF16),
            turned,
        ],
        cost=pl.CostEstimate(flops=int(PROJECT_FLOPS), bytes_accessed=1, transcendentals=0),
    )
    message, filters = after(message, filters)
    signal = exchange(message)
    (conv,) = call(
        conv_kernel, [shape((seq_count, 80, width), BF16)], signal, gain, forward, mix, twiddle, backward
    )
    columns = [around(column, steps) for column, steps in zip(columns, (1, 2, 3))]
    conv, *columns = after(conv, *columns)
    conv = exchange(conv)
    gated, mine, theirs = call(
        gate_kernel,
        [shape((rows, width), BF16)] + [shape((4 * width, width), BF16)] * 2,
        chan_index,
        conv,
        gate,
        out_weight,
        *columns,
        scalars=1,
        scratch=[turned],
    )
    moved = {steps: around(gated, steps) for steps in (1, 3, 2)}
    pieces = [gated] + [moved[steps] for steps in (1, 2, 3)]
    theirs, pieces[3] = after(across(theirs), pieces[3])
    pieces = pieces + [across(piece) for piece in pieces]
    (result,) = call(
        output_kernel,
        [shape((rows, width), F32)],
        *pieces,
        mine,
        theirs,
        tokens,
        written=(0,),
        scratch=[turned, pltpu.SemaphoreType.DMA((rows // 256,))],
    )
    return result


def solution(mesh):
    return jax.shard_map(
        local,
        mesh=mesh,
        in_specs=(
            P("seq", "chan"),
            P(),
            P(None, None, "chan"),
            P(None, None, "chan"),
            P("seq", "chan"),
            P("seq", "chan"),
            P("chan"),
            P("chan", None),
        ),
        out_specs=P("seq", "chan"),
        check_vma=False,
    )
```
